256 devices in a mesh: row: 8 (over y, core), col: 8 (over x, z_lo), aux: 4 (over z_hi).
Axes of the slice: x: 4, y: 4, z: 8 (z_hi: 4, z_lo: 2; z = z_hi * 2 + z_lo), core: 2. Of those that a mesh axis runs over, the one named last changes fastest.
Arguments:
- slabs: bfloat16 [5056, 32, 512], P('row', 'col', 'aux'), may hold values from -6 to 6
- gammas: bfloat16 [5056, 32, 512], P('row', 'col', 'aux'), may hold values from -0.046875 to 0.046875
- occupied: int32 [5056], replicated, may hold values 0 or 1
- energies: float32 [5056], replicated, may hold values from -2 to 2
Outputs:
- gradient: float32 [5056, 5056], P(('row', 'aux'), 'col')
- rotation_step: float32 [5056, 5056], P(('row', 'aux'), 'col')
The draws below stay inside these ranges and needn't reach their ends.
All inputs are finite; a program needn't handle non-finite values.
Results may differ from the reference program's by a relative error of at most 0.0003.
Values may be sent and summed in bfloat16 or wider, within the bound.
A program may use at most 128 MiB of HBM per device.

```python
import jax
import jax.numpy as jnp

NORB = 5056
NAUX = 512
RWIN = 32


def with_ends(drawn, rng, least, largest):
    dims = drawn.shape
    index_at = [jax.random.randint(jax.random.fold_in(rng, axis), (), 0, dims[axis]) for axis in range(len(dims))]
    drawn = drawn.at[tuple(index_at)].set(least)
    longest = dims.index(max(dims))
    index_at[longest] = (index_at[longest] + 1) % dims[longest]
    return drawn.at[tuple(index_at)].set(largest)


def block_scale(stream_key, dims, split, least, largest):
    def one(position, shards_of):
        draws = jax.random.uniform(jax.random.fold_in(jax.random.fold_in(stream_key, 6), position), (shards_of,), jnp.float32, least / len(split), largest / len(split))
        return jnp.repeat(jnp.exp(draws), dims[position] // shards_of).reshape((-1,) + (1,) * (len(dims) - position - 1))

    factor_of = one(*split[0])
    for cut in split[1:]:
        factor_of = factor_of * one(*cut)
    return factor_of


def centred(own_key, dims, scale, bound, split=(), dtype=jnp.bfloat16):
    values = scale * jax.random.normal(own_key, dims, jnp.float32)
    if split:
        values = values * block_scale(own_key, dims, split, -0.22, 0.18)
    return jnp.clip(values, -bound, bound).astype(dtype)


def setup_inputs(seed: int = 0) -> dict:
    keys = jax.random.split(jax.random.key(seed), 5)
    return {
        "slabs": centred(keys[0], (NORB, RWIN, NAUX), 1.0, 6.0, ((0, 8), (1, 8), (2, 4))),
        "gammas": centred(keys[1], (NORB, RWIN, NAUX), (NAUX * RWIN) ** -0.5, 0.046875, ((0, 8), (1, 8), (2, 4))),
        "occupied": with_ends((jax.random.randint(keys[2], (NORB,), 0, 4) < 1).astype(jnp.int32), jax.random.fold_in(keys[2], 1), 0, 1),
        "energies": jnp.clip(jax.random.uniform(keys[3], (NORB,), jnp.float32, -2.0, 2.0), -2.0, 2.0),
    }


def reference(slabs, gammas, occupied, energies):
    flat_slabs = slabs.reshape(NORB, RWIN * NAUX)
    flat_gammas = gammas.reshape(NORB, RWIN * NAUX)
    fock_total = jnp.dot(flat_slabs, flat_gammas.T, preferred_element_type=jnp.float32)
    gradient = 2.0 * (fock_total - fock_total.T)
    nonredundant = occupied[:, None] + occupied[None, :] - 2 * occupied[:, None] * occupied[None, :]
    denominator = 4.0 * jnp.abs(energies[:, None] - energies[None, :]) + 0.5
    rotation_step = -nonredundant.astype(jnp.float32) * gradient / denominator
    return gradient, rotation_step
```

```python
import functools

import jax
import jax.numpy as jnp
from jax import lax
from jax.experimental import pallas as pl
from jax.experimental.pallas import tpu as pltpu
from jax.sharding import PartitionSpec as P

SUB = 160
STEPS = 2
CH = SUB // STEPS
HALF = CH // 2
WIDE = 4 * SUB
KX = 512
PIECE = 256


def kernel(s_ref, g_ref, direct, mirror, sbuf, gbuf, fock, rs_half, rs_full, send, recv, loc):
    row, col, aux = lax.axis_index("row"), lax.axis_index("col"), lax.axis_index("aux")
    y, c = row // 2, row % 2
    x, zlo = col // 2, col % 2
    z = 2 * aux + zlo

    def at(row_=row, col_=col, aux_=aux):
        return {"row": row_, "col": col_, "aux": aux_}

    def x_at(d):
        return at(col_=2 * ((x + d) % 4) + zlo)

    def y_at(d):
        return at(row_=2 * ((y + d) % 4) + c)

    def z_at(d):
        there = (z + d) % 8
        return at(col_=2 * x + there % 2, aux_=there // 2)

    other = at(row_=2 * y + (1 - c))

    sends = []
    count = [0]

    def slot():
        count[0] += 1
        return count[0] - 1

    def put(n, src, dst, dev):
        copy = pltpu.make_async_remote_copy(
            src_ref=src, dst_ref=dst, send_sem=send.at[n], recv_sem=recv.at[n],
            device_id=dev, device_id_type=pl.DeviceIdType.MESH)
        copy.start()
        sends.append(copy)

    def got(n, dst, dev):
        pltpu.make_async_remote_copy(
            src_ref=dst, dst_ref=dst, send_sem=send.at[n], recv_sem=recv.at[n],
            device_id=dev, device_id_type=pl.DeviceIdType.MESH).wait_recv()

    def mirror_from(r):
        return at(2 * x + zlo, 2 * aux + c, r)

    def mirror_to(t):
        return at(2 * t + zlo, 2 * y + c, x)

    on_diagonal = jnp.logical_and(jnp.logical_and(zlo == c, x == y), aux == x)

    barrier = pltpu.get_barrier_semaphore()

    def greet(dev):
        pl.semaphore_signal(barrier, inc=1, device_id=dev, device_id_type=pl.DeviceIdType.MESH)

    for dev in (x_at(1), x_at(3), x_at(2), y_at(1), y_at(3), other, z_at(1), z_at(7)):
        greet(dev)
    for r in range(4):
        mine = jnp.logical_and(on_diagonal, aux == r)

        @pl.when(jnp.logical_not(mine))
        def _():
            greet(mirror_from(r))

    pl.semaphore_wait(barrier, 12 - on_diagonal.astype(jnp.int32))

    lanes = [pl.ds(KX * p, KX) for p in range(4)]

    a2a = [None] + [slot() for _ in range(3)]
    for d in (1, 3, 2):
        put(a2a[d], g_ref.at[(x + d) % 4], gbuf.at[c, y, :, lanes[(4 - d) % 4]], x_at(d))
    gbuf[c, y, :, 0:KX] = g_ref[x]

    s_plus = [slot() for _ in range(STEPS)]
    s_minus = [slot() for _ in range(STEPS)]
    s_fwd = [[slot(), slot()] for _ in range(STEPS)]
    rows_half = 2 * CH

    def send_rows(h):
        put(s_plus[h], s_ref.at[h], sbuf.at[h, :, lanes[3]], x_at(1))
        put(s_minus[h], s_ref.at[h], sbuf.at[h, :, lanes[1]], x_at(3))

    def forward_rows(h):
        low, high = pl.ds(0, rows_half), pl.ds(rows_half, rows_half)
        got(s_plus[h], sbuf.at[h, :, lanes[3]], x_at(3))
        put(s_fwd[h][0], sbuf.at[h, low, lanes[3]], sbuf.at[h, low, lanes[2]], x_at(1))
        got(s_minus[h], sbuf.at[h, :, lanes[1]], x_at(1))
        put(s_fwd[h][1], sbuf.at[h, high, lanes[1]], sbuf.at[h, high, lanes[2]], x_at(3))

    def finish_rows(h):
        low, high = pl.ds(0, rows_half), pl.ds(rows_half, rows_half)
        got(s_fwd[h][0], sbuf.at[h, low, lanes[2]], x_at(3))
        got(s_fwd[h][1], sbuf.at[h, high, lanes[2]], x_at(1))

    y_plus = [slot() for _ in range(4)]
    y_minus = [slot() for _ in range(4)]
    y_far = [slot() for _ in range(4)]
    cross = [[slot() for _ in range(4)] for _ in range(4)]

    def piece(core, yy, p):
        return gbuf.at[core, yy, :, lanes[p]]

    def over(d, p):
        yy = (y + d) % 4
        put(cross[d][p], piece(c, yy, p), piece(c, yy, p), other)

    def spread(p):
        put(y_plus[p], piece(c, y, p), piece(c, y, p), y_at(1))
        put(y_minus[p], piece(c, y, p), piece(c, y, p), y_at(3))
        over(0, p)

    def relay(p):
        below, above = (y + 3) % 4, (y + 1) % 4
        got(y_plus[p], piece(c, below, p), y_at(3))
        if p in (0, 1):
            put(y_far[p], piece(c, below, p), piece(c, below, p), y_at(1))
        over(3, p)
        got(y_minus[p], piece(c, above, p), y_at(1))
        if p in (2, 3):
            put(y_far[p], piece(c, above, p), piece(c, above, p), y_at(3))
        over(1, p)

    def relay_far(p):
        got(y_far[p], piece(c, (y + 2) % 4, p), y_at(3) if p in (0, 1) else y_at(1))
        over(2, p)

    spread(0)
    for h in range(STEPS):
        send_rows(h)
        sbuf[h, :, 0:KX] = s_ref[h]
    for d in (1, 3, 2):
        p = (4 - d) % 4
        got(a2a[d], piece(c, y, p), x_at(4 - d))
        spread(p)
    relay(0)
    relay(3)
    relay(1)
    forward_rows(0)
    relay(2)
    for p in (0, 3, 1, 2):
        relay_far(p)
    for d in range(4):
        for p in range(4):
            got(cross[d][p], piece(1 - c, (y + d) % 4, p), other)

    rs_send = [[[slot() for _ in range(4)] for _ in range(2)] for _ in range(STEPS)]

    def multiply(h):
        def column_block(cc, carry):
            out = lax.dot_general(
                sbuf[h], gbuf[cc].reshape(WIDE, 4 * KX), (((1,), (1,)), ((), ())),
                preferred_element_type=jnp.float32)
            fock[h, :, cc] = out.reshape(4, CH, WIDE)
            return carry

        lax.fori_loop(0, 2, column_block, 0)

    def chunk(h, d):
        there = (z + d) % 8
        return h, there // 2, there % 2

    halves = (pl.ds(0, HALF), pl.ds(HALF, HALF))

    def reduce_step(h, t):
        for way in range(2):
            sign = 1 if way == 0 else 7
            nxt, prev = z_at(sign), z_at(8 - sign)
            here = chunk(h, sign * (4 - t))
            if t == 0:
                put(rs_send[h][way][0], fock.at[(*here, halves[way])], rs_half.at[way, h], nxt)
                continue
            if t == 1:
                got(rs_send[h][way][0], rs_half.at[way, h], prev)
                fock[(*here, halves[way])] += rs_half[way, h]
            else:
                got(rs_send[h][way][t - 1], rs_full.at[way, h, t - 2], prev)
                fock[here] += rs_full[way, h, t - 2]
            if t < 4:
                put(rs_send[h][way][t], fock.at[here], rs_full.at[way, h, t - 1], nxt)

    for h in range(STEPS):
        if h > 0:
            forward_rows(h)
        finish_rows(h)
        multiply(h)
        reduce_step(h, 0)
    for t in range(1, 5):
        for h in range(STEPS):
            reduce_step(h, t)

    x_out = [[slot() for _ in range(3)] for _ in range(STEPS)]
    m_out = [[slot() for _ in range(4)] for _ in range(STEPS)]
    for h in range(STEPS):
        rows = pl.ds(CH * h, CH)
        mine = fock.at[h, aux, zlo]

        def lanes_of(t):
            return pl.ds(pl.multiple_of(128 * t, 128), PIECE)

        for d in (1, 2, 3):
            put(x_out[h][d - 1], mine.at[:, lanes_of((x + d) % 4)], direct.at[x, rows], x_at(d))
        for t in range(4):
            copy_args = (mine.at[:, lanes_of(t)], mirror.at[aux, rows])
            here = jnp.logical_and(on_diagonal, y == t)

            @pl.when(here)
            def _():
                local = pltpu.make_async_copy(*copy_args, loc.at[STEPS + h])
                local.start()
                local.wait()

            @pl.when(jnp.logical_not(here))
            def _():
                pltpu.make_async_remote_copy(
                    src_ref=copy_args[0], dst_ref=copy_args[1],
                    send_sem=send.at[m_out[h][t]], recv_sem=recv.at[m_out[h][0] + aux],
                    device_id=mirror_to(t), device_id_type=pl.DeviceIdType.MESH).start()
        local = pltpu.make_async_copy(mine.at[:, lanes_of(x)], direct.at[x, rows], loc.at[h])
        local.start()
        local.wait()

    for h in range(STEPS):
        rows = pl.ds(CH * h, CH)
        for d in (1, 2, 3):
            got(x_out[h][d - 1], direct.at[(x + 4 - d) % 4, rows], x_at(4 - d))
        for r in range(4):
            @pl.when(jnp.logical_not(jnp.logical_and(on_diagonal, aux == r)))
            def _():
                got(m_out[h][r], mirror.at[r, rows], mirror_from(r))

    for copy in sends:
        copy.wait_send()
    for h in range(STEPS):
        rows = pl.ds(CH * h, CH)
        for t in range(4):
            @pl.when(jnp.logical_not(jnp.logical_and(on_diagonal, y == t)))
            def _():
                pltpu.make_async_remote_copy(
                    src_ref=fock.at[h, aux, zlo, :, pl.ds(0, PIECE)], dst_ref=mirror.at[aux, rows],
                    send_sem=send.at[m_out[h][t]], recv_sem=recv.at[m_out[h][0] + aux],
                    device_id=mirror_to(t), device_id_type=pl.DeviceIdType.MESH).wait_send()


COPIES = 3 + 4 * STEPS + 12 + 16 + 8 * STEPS + 7 * STEPS


def exchange(slabs, gammas):
    vmem = pl.BlockSpec(memory_space=pltpu.VMEM)
    out = jax.ShapeDtypeStruct((4, SUB, PIECE), jnp.float32)
    return pl.pallas_call(
        kernel,
        out_shape=(out, out),
        in_specs=[vmem, vmem],
        out_specs=(vmem, vmem),
        scratch_shapes=[
            pltpu.VMEM((STEPS, 4 * CH, 4 * KX), jnp.bfloat16),
            pltpu.VMEM((2, 4, SUB, 4 * KX), jnp.bfloat16),
            pltpu.VMEM((STEPS, 4, 2, CH, WIDE), jnp.float32),
            pltpu.VMEM((2, STEPS, HALF, WIDE), jnp.float32),
            pltpu.VMEM((2, STEPS, 3, CH, WIDE), jnp.float32),
            pltpu.SemaphoreType.DMA((COPIES,)),
            pltpu.SemaphoreType.DMA((COPIES,)),
            pltpu.SemaphoreType.DMA((2 * STEPS,)),
        ],
        compiler_params=pltpu.CompilerParams(
            collective_id=0, has_side_effects=True, vmem_limit_bytes=48 * 1024 * 1024),
        cost_estimate=pl.CostEstimate(
            flops=2 * 640 * 1280 * 2048, bytes_accessed=4 * 1024 * 1024, transcendentals=0),
    )(slabs, gammas)


def on_device(slabs, gammas, occupied, energies):
    block = slabs.shape[0]
    sub = block // 4

    def pieces(a):
        return jnp.pad(a.reshape(4, sub, KX), ((0, 0), (0, SUB - sub), (0, 0)))

    row, col, aux = lax.axis_index("row"), lax.axis_index("col"), lax.axis_index("aux")
    s = pieces(slabs).reshape(4, STEPS, CH, KX).transpose(1, 0, 2, 3).reshape(STEPS, 4 * CH, KX)
    direct, mirror = exchange(s, pieces(gammas))
    own = lax.dynamic_slice_in_dim(direct[:, :sub], 32 * (col // 2), sub, axis=2)
    other = lax.dynamic_slice_in_dim(mirror[:, :sub], 32 * (row // 2), sub, axis=2)
    own = own.transpose(1, 0, 2).reshape(sub, block)
    other = other.reshape(block, sub).T
    gradient = 2.0 * (own - other)
    row_start = row * block + aux * sub
    col_start = col * block
    energy_rows = lax.dynamic_slice_in_dim(energies, row_start, sub)
    energy_cols = lax.dynamic_slice_in_dim(energies, col_start, block)
    occ_rows = lax.dynamic_slice_in_dim(occupied, row_start, sub)
    occ_cols = lax.dynamic_slice_in_dim(occupied, col_start, block)
    nonredundant = occ_rows[:, None] + occ_cols[None, :] - 2 * occ_rows[:, None] * occ_cols[None, :]
    denominator = 4.0 * jnp.abs(energy_rows[:, None] - energy_cols[None, :]) + 0.5
    rotation_step = -nonredundant.astype(jnp.float32) * gradient / denominator
    return (gradient, rotation_step)


def solution(mesh):
    placed = (P("row", "col", "aux"), P("row", "col", "aux"), P(), P())
    return jax.shard_map(
        on_device,
        mesh=mesh,
        in_specs=placed,
        out_specs=(P(("row", "aux"), "col"), P(("row", "aux"), "col")),
        check_vma=False,
    )
```

```python
import functools

import jax
import jax.numpy as jnp
from jax import lax
from jax.experimental import pallas as pl
from jax.experimental.pallas import tpu as pltpu
from jax.sharding import PartitionSpec as P

SUB = 160
STEPS = 2
CH = SUB // STEPS
HALF = CH // 2
WIDE = 4 * SUB
KX = 512
PIECE = 256


def kernel(s_ref, g_ref, direct, mirror, sbuf, gbuf, fock, rs_half, rs_full, by_y, by_x, send, recv, loc):
    row, col, aux = lax.axis_index("row"), lax.axis_index("col"), lax.axis_index("aux")
    y, c = row // 2, row % 2
    x, zlo = col // 2, col % 2
    z = 2 * aux + zlo

    def at(row_=row, col_=col, aux_=aux):
        return {"row": row_, "col": col_, "aux": aux_}

    def x_at(d):
        return at(col_=2 * ((x + d) % 4) + zlo)

    def y_at(d):
        return at(row_=2 * ((y + d) % 4) + c)

    def z_at(d):
        there = (z + d) % 8
        return at(col_=2 * x + there % 2, aux_=there // 2)

    other = at(row_=2 * y + (1 - c))

    sends = []
    count = [0]

    def slot():
        count[0] += 1
        return count[0] - 1

    def put(n, src, dst, dev):
        copy = pltpu.make_async_remote_copy(
            src_ref=src, dst_ref=dst, send_sem=send.at[n], recv_sem=recv.at[n],
            device_id=dev, device_id_type=pl.DeviceIdType.MESH)
        copy.start()
        sends.append(copy)

    def got(n, dst, dev):
        pltpu.make_async_remote_copy(
            src_ref=dst, dst_ref=dst, send_sem=send.at[n], recv_sem=recv.at[n],
            device_id=dev, device_id_type=pl.DeviceIdType.MESH).wait_recv()

    def swapped(m):
        return at(2 * y + zlo, 2 * x + c, m)

    same_core = zlo == c

    barrier = pltpu.get_barrier_semaphore()

    def greet(dev):
        pl.semaphore_signal(barrier, inc=1, device_id=dev, device_id_type=pl.DeviceIdType.MESH)

    for dev in (x_at(1), x_at(3), x_at(2), y_at(1), y_at(3), y_at(2), other, z_at(1), z_at(7)):
        greet(dev)
    for r in range(4):
        @pl.when(jnp.logical_not(jnp.logical_and(same_core, aux == r)))
        def _():
            greet(swapped(r))

    pl.semaphore_wait(barrier, 13 - same_core.astype(jnp.int32))

    lanes = [pl.ds(KX * p, KX) for p in range(4)]

    a2a = [None] + [slot() for _ in range(3)]
    for d in (1, 3, 2):
        put(a2a[d], g_ref.at[(x + d) % 4], gbuf.at[c, y, :, lanes[(4 - d) % 4]], x_at(d))
    gbuf[c, y, :, 0:KX] = g_ref[x]

    s_plus = [slot() for _ in range(STEPS)]
    s_minus = [slot() for _ in range(STEPS)]
    s_fwd = [[slot(), slot()] for _ in range(STEPS)]
    rows_half = 2 * CH

    def send_rows(h):
        put(s_plus[h], s_ref.at[h], sbuf.at[h, :, lanes[3]], x_at(1))
        put(s_minus[h], s_ref.at[h], sbuf.at[h, :, lanes[1]], x_at(3))

    def forward_rows(h):
        low, high = pl.ds(0, rows_half), pl.ds(rows_half, rows_half)
        got(s_plus[h], sbuf.at[h, :, lanes[3]], x_at(3))
        put(s_fwd[h][0], sbuf.at[h, low, lanes[3]], sbuf.at[h, low, lanes[2]], x_at(1))
        got(s_minus[h], sbuf.at[h, :, lanes[1]], x_at(1))
        put(s_fwd[h][1], sbuf.at[h, high, lanes[1]], sbuf.at[h, high, lanes[2]], x_at(3))

    def finish_rows(h):
        low, high = pl.ds(0, rows_half), pl.ds(rows_half, rows_half)
        got(s_fwd[h][0], sbuf.at[h, low, lanes[2]], x_at(3))
        got(s_fwd[h][1], sbuf.at[h, high, lanes[2]], x_at(1))

    y_plus = [slot() for _ in range(4)]
    y_minus = [slot() for _ in range(4)]
    y_far = [slot() for _ in range(4)]
    cross = [[slot() for _ in range(4)] for _ in range(4)]

    def piece(core, yy, p):
        return gbuf.at[core, yy, :, lanes[p]]

    def over(d, p):
        yy = (y + d) % 4
        put(cross[d][p], piece(c, yy, p), piece(c, yy, p), other)

    def spread(p):
        put(y_plus[p], piece(c, y, p), piece(c, y, p), y_at(1))
        put(y_minus[p], piece(c, y, p), piece(c, y, p), y_at(3))
        over(0, p)

    def relay(p):
        below, above = (y + 3) % 4, (y + 1) % 4
        got(y_plus[p], piece(c, below, p), y_at(3))
        if p in (0, 1):
            put(y_far[p], piece(c, below, p), piece(c, below, p), y_at(1))
        over(3, p)
        got(y_minus[p], piece(c, above, p), y_at(1))
        if p in (2, 3):
            put(y_far[p], piece(c, above, p), piece(c, above, p), y_at(3))
        over(1, p)

    def relay_far(p):
        got(y_far[p], piece(c, (y + 2) % 4, p), y_at(3) if p in (0, 1) else y_at(1))
        over(2, p)

    spread(0)
    for h in range(STEPS):
        send_rows(h)
        sbuf[h, :, 0:KX] = s_ref[h]
    for d in (1, 3, 2):
        p = (4 - d) % 4
        got(a2a[d], piece(c, y, p), x_at(4 - d))
        spread(p)
    relay(0)
    relay(3)
    relay(1)
    forward_rows(0)
    relay(2)
    for p in (0, 3, 1, 2):
        relay_far(p)
    for d in range(4):
        for p in range(4):
            got(cross[d][p], piece(1 - c, (y + d) % 4, p), other)

    rs_send = [[[slot() for _ in range(4)] for _ in range(2)] for _ in range(STEPS)]

    def multiply(h):
        def column_block(cc, carry):
            out = lax.dot_general(
                sbuf[h], gbuf[cc].reshape(WIDE, 4 * KX), (((1,), (1,)), ((), ())),
                preferred_element_type=jnp.float32)
            fock[h, :, cc] = out.reshape(4, CH, WIDE)
            return carry

        lax.fori_loop(0, 2, column_block, 0)

    def chunk(h, d):
        there = (z + d) % 8
        return h, there // 2, there % 2

    halves = (pl.ds(0, HALF), pl.ds(HALF, HALF))

    def reduce_step(h, t):
        for way in range(2):
            sign = 1 if way == 0 else 7
            nxt, prev = z_at(sign), z_at(8 - sign)
            here = chunk(h, sign * (4 - t))
            if t == 0:
                put(rs_send[h][way][0], fock.at[(*here, halves[way])], rs_half.at[way, h], nxt)
                continue
            if t == 1:
                got(rs_send[h][way][0], rs_half.at[way, h], prev)
                fock[(*here, halves[way])] += rs_half[way, h]
            else:
                got(rs_send[h][way][t - 1], rs_full.at[way, h, t - 2], prev)
                fock[here] += rs_full[way, h, t - 2]
            if t < 4:
                put(rs_send[h][way][t], fock.at[here], rs_full.at[way, h, t - 1], nxt)

    for h in range(STEPS):
        if h > 0:
            forward_rows(h)
        finish_rows(h)
        multiply(h)
        reduce_step(h, 0)
    x_out = [[slot() for _ in range(3)] for _ in range(STEPS)]
    y_out = [[slot() for _ in range(3)] for _ in range(STEPS)]
    t_out = [[slot() for _ in range(4)] for _ in range(STEPS)]
    m_out = [[slot() for _ in range(4)] for _ in range(STEPS)]

    def rows_of(h):
        return pl.ds(CH * h, CH)

    def lanes_of(t):
        return pl.ds(pl.multiple_of(128 * t, 128), PIECE)

    def local(n, src, dst):
        return pltpu.make_async_copy(src, dst, loc.at[n])

    def remote(n_send, n_recv, src, dst, dev):
        return pltpu.make_async_remote_copy(
            src_ref=src, dst_ref=dst, send_sem=send.at[n_send], recv_sem=recv.at[n_recv],
            device_id=dev, device_id_type=pl.DeviceIdType.MESH)

    def leave(h):
        mine = fock.at[h, aux, zlo]
        for d in (2, 1, 3):
            put(y_out[h][d - 1], mine.at[:, lanes_of((y + d) % 4)], by_y.at[h, y], y_at(d))
        for d in (2, 1, 3):
            put(x_out[h][d - 1], mine.at[:, lanes_of((x + d) % 4)], direct.at[x, rows_of(h)], x_at(d))
        copies = (local(4 * h, mine.at[:, lanes_of(y)], by_y.at[h, y]),
                  local(4 * h + 1, mine.at[:, lanes_of(x)], direct.at[x, rows_of(h)]))
        for copy in copies:
            copy.start()
        for copy in copies:
            copy.wait()

    def along_x(h, d):
        t = (y + d) % 4
        return remote(t_out[h][d], t_out[h][0] + x, by_y.at[h, t], by_x.at[h, x], at(col_=2 * t + zlo))

    def along_z(h, m):
        return remote(m_out[h][m], m_out[h][0] + aux, by_x.at[h, m], mirror.at[aux, rows_of(h)], swapped(m))

    def turn(h):
        for d in (0, 1, 3, 2):
            t = (y + d) % 4
            if d:
                got(y_out[h][3 - d], by_y.at[h, t], y_at(d))

            @pl.when(t == x)
            def _():
                copy = local(4 * h + 2, by_y.at[h, t], by_x.at[h, x])
                copy.start()
                copy.wait()

            @pl.when(t != x)
            def _():
                along_x(h, d).start()

    def swap(h):
        for m in range(4):
            @pl.when(m != x)
            def _():
                got(t_out[h][m], by_x.at[h, m], at(col_=2 * m + zlo))

            here = jnp.logical_and(same_core, aux == m)

            @pl.when(here)
            def _():
                copy = local(4 * h + 3, by_x.at[h, m], mirror.at[aux, rows_of(h)])
                copy.start()
                copy.wait()

            @pl.when(jnp.logical_not(here))
            def _():
                along_z(h, m).start()

    def arrive(h):
        for d in (1, 2, 3):
            got(x_out[h][d - 1], direct.at[(x + 4 - d) % 4, rows_of(h)], x_at(4 - d))
        for r in range(4):
            @pl.when(jnp.logical_not(jnp.logical_and(same_core, aux == r)))
            def _():
                got(m_out[h][r], mirror.at[r, rows_of(h)], swapped(r))

    for t in range(1, 5):
        for h in range(STEPS):
            reduce_step(h, t)
            if t == 4:
                leave(h)
                if h > 0:
                    turn(h - 1)
    turn(STEPS - 1)
    for h in range(STEPS):
        swap(h)
    for h in range(STEPS):
        arrive(h)
    for copy in sends:
        copy.wait_send()
    for h in range(STEPS):
        for d in range(4):
            @pl.when((y + d) % 4 != x)
            def _():
                along_x(h, d).wait_send()
        for m in range(4):
            @pl.when(jnp.logical_not(jnp.logical_and(same_core, aux == m)))
            def _():
                along_z(h, m).wait_send()


COPIES = 3 + 4 * STEPS + 12 + 16 + 8 * STEPS + 14 * STEPS


def exchange(slabs, gammas):
    vmem = pl.BlockSpec(memory_space=pltpu.VMEM)
    out = jax.ShapeDtypeStruct((4, SUB, PIECE), jnp.float32)
    return pl.pallas_call(
        kernel,
        out_shape=(out, out),
        in_specs=[vmem, vmem],
        out_specs=(vmem, vmem),
        scratch_shapes=[
            pltpu.VMEM((STEPS, 4 * CH, 4 * KX), jnp.bfloat16),
            pltpu.VMEM((2, 4, SUB, 4 * KX), jnp.bfloat16),
            pltpu.VMEM((STEPS, 4, 2, CH, WIDE), jnp.float32),
            pltpu.VMEM((2, STEPS, HALF, WIDE), jnp.float32),
            pltpu.VMEM((2, STEPS, 3, CH, WIDE), jnp.float32),
            pltpu.VMEM((STEPS, 4, CH, PIECE), jnp.float32),
            pltpu.VMEM((STEPS, 4, CH, PIECE), jnp.float32),
            pltpu.SemaphoreType.DMA((COPIES,)),
            pltpu.SemaphoreType.DMA((COPIES,)),
            pltpu.SemaphoreType.DMA((4 * STEPS,)),
        ],
        compiler_params=pltpu.CompilerParams(
            collective_id=0, has_side_effects=True, vmem_limit_bytes=48 * 1024 * 1024),
        cost_estimate=pl.CostEstimate(
            flops=2 * 640 * 1280 * 2048, bytes_accessed=4 * 1024 * 1024, transcendentals=0),
    )(slabs, gammas)


def on_device(slabs, gammas, occupied, energies):
    block = slabs.shape[0]
    sub = block // 4

    def pieces(a):
        return jnp.pad(a.reshape(4, sub, KX), ((0, 0), (0, SUB - sub), (0, 0)))

    row, col, aux = lax.axis_index("row"), lax.axis_index("col"), lax.axis_index("aux")
    s = pieces(slabs).reshape(4, STEPS, CH, KX).transpose(1, 0, 2, 3).reshape(STEPS, 4 * CH, KX)
    direct, mirror = exchange(s, pieces(gammas))
    own = lax.dynamic_slice_in_dim(direct[:, :sub], 32 * (col // 2), sub, axis=2)
    other = lax.dynamic_slice_in_dim(mirror[:, :sub], 32 * (row // 2), sub, axis=2)
    own = own.transpose(1, 0, 2).reshape(sub, block)
    other = other.reshape(block, sub).T
    gradient = 2.0 * (own - other)
    row_start = row * block + aux * sub
    col_start = col * block
    energy_rows = lax.dynamic_slice_in_dim(energies, row_start, sub)
    energy_cols = lax.dynamic_slice_in_dim(energies, col_start, block)
    occ_rows = lax.dynamic_slice_in_dim(occupied, row_start, sub)
    occ_cols = lax.dynamic_slice_in_dim(occupied, col_start, block)
    nonredundant = occ_rows[:, None] + occ_cols[None, :] - 2 * occ_rows[:, None] * occ_cols[None, :]
    denominator = 4.0 * jnp.abs(energy_rows[:, None] - energy_cols[None, :]) + 0.5
    rotation_step = -nonredundant.astype(jnp.float32) * gradient / denominator
    return (gradient, rotation_step)


def solution(mesh):
    placed = (P("row", "col", "aux"), P("row", "col", "aux"), P(), P())
    return jax.shard_map(
        on_device,
        mesh=mesh,
        in_specs=placed,
        out_specs=(P(("row", "aux"), "col"), P(("row", "aux"), "col")),
        check_vma=False,
    )
```

```python
import functools

import jax
import jax.numpy as jnp
from jax import lax
from jax.experimental import pallas as pl
from jax.experimental.pallas import tpu as pltpu
from jax.sharding import PartitionSpec as P

SUB = 160
STEPS = 2
CH = SUB // STEPS
LAST = CH - 1
WIDE = 4 * SUB
KX = 512
PIECE = 256
TOP = 32760.0
FINE = 128.0


def encode(v):
    inside = lax.broadcasted_iota(jnp.int32, v.shape, 0) < LAST
    size = jnp.where(inside, jnp.abs(v), 0.0)
    largest = jnp.maximum(jnp.max(size, axis=0, keepdims=True), 1e-30)
    scale = jnp.ceil(jnp.log2(largest) * FINE)
    code = (jnp.sqrt(size) * (jnp.exp2(scale * (-0.5 / FINE)) * TOP) + 0.5).astype(jnp.int32)
    code = jnp.where(v < 0.0, -code, code)
    return jnp.where(inside, code, scale.astype(jnp.int32)).astype(jnp.int16)


def decode(code):
    value = code.astype(jnp.int32).astype(jnp.float32)
    root = value * (jnp.exp2(value[LAST:CH] * (0.5 / FINE)) * (1.0 / TOP))
    return root * jnp.abs(root)


def kernel(s_ref, g_ref, direct, mirror, sbuf, gbuf, fock, out_codes, in_codes, reduced, direct_codes, mirror_codes,
           by_y, by_x, send, recv, loc):
    row, col, aux = lax.axis_index("row"), lax.axis_index("col"), lax.axis_index("aux")
    y, c = row // 2, row % 2
    x, zlo = col // 2, col % 2
    z = 2 * aux + zlo

    def at(row_=row, col_=col, aux_=aux):
        return {"row": row_, "col": col_, "aux": aux_}

    def x_at(d):
        return at(col_=2 * ((x + d) % 4) + zlo)

    def y_at(d):
        return at(row_=2 * ((y + d) % 4) + c)

    def z_at(d):
        there = (z + d) % 8
        return at(col_=2 * x + there % 2, aux_=there // 2)

    other = at(row_=2 * y + (1 - c))

    sends = []
    count = [0]

    def slot():
        count[0] += 1
        return count[0] - 1

    def put(n, src, dst, dev):
        copy = pltpu.make_async_remote_copy(
            src_ref=src, dst_ref=dst, send_sem=send.at[n], recv_sem=recv.at[n],
            device_id=dev, device_id_type=pl.DeviceIdType.MESH)
        copy.start()
        sends.append(copy)

    def got(n, dst, dev):
        pltpu.make_async_remote_copy(
            src_ref=dst, dst_ref=dst, send_sem=send.at[n], recv_sem=recv.at[n],
            device_id=dev, device_id_type=pl.DeviceIdType.MESH).wait_recv()

    def swapped(m):
        return at(2 * y + zlo, 2 * x + c, m)

    same_core = zlo == c

    barrier = pltpu.get_barrier_semaphore()

    def greet(dev):
        pl.semaphore_signal(barrier, inc=1, device_id=dev, device_id_type=pl.DeviceIdType.MESH)

    for dev in (x_at(1), x_at(3), x_at(2), y_at(1), y_at(3), y_at(2), other, z_at(1), z_at(7)):
        greet(dev)
    for r in range(4):
        @pl.when(jnp.logical_not(jnp.logical_and(same_core, aux == r)))
        def _():
            greet(swapped(r))

    pl.semaphore_wait(barrier, 13 - same_core.astype(jnp.int32))

    lanes = [pl.ds(KX * p, KX) for p in range(4)]

    a2a = [None] + [slot() for _ in range(3)]
    for d in (1, 3, 2):
        put(a2a[d], g_ref.at[(x + d) % 4], gbuf.at[c, y, :, lanes[(4 - d) % 4]], x_at(d))
    gbuf[c, y, :, 0:KX] = g_ref[x]

    s_plus = [slot() for _ in range(STEPS)]
    s_minus = [slot() for _ in range(STEPS)]
    s_fwd = [[slot(), slot()] for _ in range(STEPS)]
    rows_half = 2 * CH

    def send_rows(h):
        put(s_plus[h], s_ref.at[h], sbuf.at[h, :, lanes[3]], x_at(1))
        put(s_minus[h], s_ref.at[h], sbuf.at[h, :, lanes[1]], x_at(3))

    def forward_rows(h):
        low, high = pl.ds(0, rows_half), pl.ds(rows_half, rows_half)
        got(s_plus[h], sbuf.at[h, :, lanes[3]], x_at(3))
        put(s_fwd[h][0], sbuf.at[h, low, lanes[3]], sbuf.at[h, low, lanes[2]], x_at(1))
        got(s_minus[h], sbuf.at[h, :, lanes[1]], x_at(1))
        put(s_fwd[h][1], sbuf.at[h, high, lanes[1]], sbuf.at[h, high, lanes[2]], x_at(3))

    def finish_rows(h):
        low, high = pl.ds(0, rows_half), pl.ds(rows_half, rows_half)
        got(s_fwd[h][0], sbuf.at[h, low, lanes[2]], x_at(3))
        got(s_fwd[h][1], sbuf.at[h, high, lanes[2]], x_at(1))

    y_plus = [slot() for _ in range(4)]
    y_minus = [slot() for _ in range(4)]
    y_far = [slot() for _ in range(4)]
    cross = [[slot() for _ in range(4)] for _ in range(4)]

    def piece(core, yy, p):
        return gbuf.at[core, yy, :, lanes[p]]

    def over(d, p):
        yy = (y + d) % 4
        put(cross[d][p], piece(c, yy, p), piece(c, yy, p), other)

    def spread(p):
        put(y_plus[p], piece(c, y, p), piece(c, y, p), y_at(1))
        put(y_minus[p], piece(c, y, p), piece(c, y, p), y_at(3))
        over(0, p)

    def relay(p):
        below, above = (y + 3) % 4, (y + 1) % 4
        got(y_plus[p], piece(c, below, p), y_at(3))
        if p in (0, 1):
            put(y_far[p], piece(c, below, p), piece(c, below, p), y_at(1))
        over(3, p)
        got(y_minus[p], piece(c, above, p), y_at(1))
        if p in (2, 3):
            put(y_far[p], piece(c, above, p), piece(c, above, p), y_at(3))
        over(1, p)

    def relay_far(p):
        got(y_far[p], piece(c, (y + 2) % 4, p), y_at(3) if p in (0, 1) else y_at(1))
        over(2, p)

    spread(0)
    for h in range(STEPS):
        sbuf[h, :, 0:KX] = s_ref[h]
    for d in (1, 3, 2):
        p = (4 - d) % 4
        got(a2a[d], piece(c, y, p), x_at(4 - d))
        spread(p)
        if d == 3:
            send_rows(0)
    relay(0)
    relay(3)
    for h in range(1, STEPS):
        send_rows(h)
    relay(1)
    forward_rows(0)
    relay(2)
    for p in (0, 3, 1, 2):
        relay_far(p)
    for d in range(4):
        for p in range(4):
            got(cross[d][p], piece(1 - c, (y + d) % 4, p), other)

    rs = [[[slot() for _ in range(4 - (h + way) % 2)] for way in range(2)] for h in range(STEPS)]

    def multiply(h):
        def column_block(cc, carry):
            out = lax.dot_general(
                sbuf[h], gbuf[cc].reshape(WIDE, 4 * KX), (((1,), (1,)), ((), ())),
                preferred_element_type=jnp.float32)
            fock[h, :, cc] = out.reshape(4, CH, WIDE)
            return carry

        lax.fori_loop(0, 2, column_block, 0)

    def chunk(h, d):
        there = (z + d) % 8
        return h, there // 2, there % 2

    def tiles(body):
        def one(i, carry):
            body(pl.ds(pl.multiple_of(128 * i, 128), 128))
            return carry

        lax.fori_loop(0, WIDE // 128, one, 0)

    def reduce_step(h, way, step):
        hops = len(rs[h][way])
        sign = 1 if way == 0 else 7
        here = chunk(h, sign * (hops - step))
        if step > 0:
            got(rs[h][way][step - 1], in_codes.at[h, way, step - 1], z_at(8 - sign))

        def one(cols):
            v = fock[(*here, slice(None), cols)]
            if step > 0:
                v += decode(in_codes[h, way, step - 1, :, cols])
            out_codes[h, way, step, :, cols] = encode(v)

        tiles(one)
        put(rs[h][way][step], out_codes.at[h, way, step], in_codes.at[h, way, step], z_at(sign))

    def reduce_last(h):
        for way in range(2):
            got(rs[h][way][-1], in_codes.at[h, way, len(rs[h][way]) - 1], z_at(7 if way == 0 else 1))

        def one(cols):
            v = fock[(*chunk(h, 0), slice(None), cols)]
            for way in range(2):
                v += decode(in_codes[h, way, len(rs[h][way]) - 1, :, cols])
            reduced[h, :, cols] = encode(v)

        tiles(one)

    for h in range(STEPS):
        if h > 0:
            forward_rows(h)
        finish_rows(h)
        multiply(h)
        for way in range(2):
            reduce_step(h, way, 0)

    x_out = [[slot() for _ in range(3)] for _ in range(STEPS)]
    y_out = [[slot() for _ in range(3)] for _ in range(STEPS)]
    t_out = [[slot() for _ in range(4)] for _ in range(STEPS)]
    m_out = [[slot() for _ in range(4)] for _ in range(STEPS)]

    def lanes_of(t):
        return pl.ds(pl.multiple_of(128 * t, 128), PIECE)

    def local(n, src, dst):
        return pltpu.make_async_copy(src, dst, loc.at[n])

    def remote(n_send, n_recv, src, dst, dev):
        return pltpu.make_async_remote_copy(
            src_ref=src, dst_ref=dst, send_sem=send.at[n_send], recv_sem=recv.at[n_recv],
            device_id=dev, device_id_type=pl.DeviceIdType.MESH)

    def leave(h):
        mine = reduced.at[h]
        for d in (2, 1, 3):
            put(y_out[h][d - 1], mine.at[:, lanes_of((y + d) % 4)], by_y.at[h, y], y_at(d))
        for d in (2, 1, 3):
            put(x_out[h][d - 1], mine.at[:, lanes_of((x + d) % 4)], direct_codes.at[x, h], x_at(d))
        copies = (local(4 * h, mine.at[:, lanes_of(y)], by_y.at[h, y]),
                  local(4 * h + 1, mine.at[:, lanes_of(x)], direct_codes.at[x, h]))
        for copy in copies:
            copy.start()
        for copy in copies:
            copy.wait()

    def along_x(h, d):
        t = (y + d) % 4
        return remote(t_out[h][d], t_out[h][0] + x, by_y.at[h, t], by_x.at[h, x], at(col_=2 * t + zlo))

    def along_z(h, m):
        return remote(m_out[h][m], m_out[h][0] + aux, by_x.at[h, m], mirror_codes.at[aux, h], swapped(m))

    def turn(h):
        for d in (0, 1, 3, 2):
            t = (y + d) % 4
            if d:
                got(y_out[h][3 - d], by_y.at[h, t], y_at(d))

            @pl.when(t == x)
            def _():
                copy = local(4 * h + 2, by_y.at[h, t], by_x.at[h, x])
                copy.start()
                copy.wait()

            @pl.when(t != x)
            def _():
                along_x(h, d).start()

    def swap(h):
        for m in range(4):
            @pl.when(m != x)
            def _():
                got(t_out[h][m], by_x.at[h, m], at(col_=2 * m + zlo))

            here = jnp.logical_and(same_core, aux == m)

            @pl.when(here)
            def _():
                copy = local(4 * h + 3, by_x.at[h, m], mirror_codes.at[aux, h])
                copy.start()
                copy.wait()

            @pl.when(jnp.logical_not(here))
            def _():
                along_z(h, m).start()

    def arrive(h):
        for d in (1, 2, 3):
            got(x_out[h][d - 1], direct_codes.at[(x + 4 - d) % 4, h], x_at(4 - d))
        for r in range(4):
            @pl.when(jnp.logical_not(jnp.logical_and(same_core, aux == r)))
            def _():
                got(m_out[h][r], mirror_codes.at[r, h], swapped(r))

    for step in range(1, 5):
        for h in range(STEPS):
            for way in range(2):
                if step < len(rs[h][way]):
                    reduce_step(h, way, step)
    for h in range(STEPS):
        reduce_last(h)
        leave(h)
        if h > 0:
            turn(h - 1)
    turn(STEPS - 1)
    for h in range(STEPS):
        swap(h)
    for h in range(STEPS):
        arrive(h)

    def unpack(i, carry):
        for h in range(STEPS):
            direct[i, h] = pltpu.roll(decode(direct_codes[i, h]), (PIECE - 32 * x) % PIECE, 1)
            mirror[i, h] = pltpu.roll(decode(mirror_codes[i, h]), (PIECE - 32 * y) % PIECE, 1)
        return carry

    lax.fori_loop(0, 4, unpack, 0)
    for copy in sends:
        copy.wait_send()
    for h in range(STEPS):
        for d in range(4):
            @pl.when((y + d) % 4 != x)
            def _():
                along_x(h, d).wait_send()
        for m in range(4):
            @pl.when(jnp.logical_not(jnp.logical_and(same_core, aux == m)))
            def _():
                along_z(h, m).wait_send()


COPIES = 3 + 4 * STEPS + 12 + 16 + 7 * STEPS + 14 * STEPS


def exchange(slabs, gammas):
    vmem = pl.BlockSpec(memory_space=pltpu.VMEM)
    out = jax.ShapeDtypeStruct((4, STEPS, CH, PIECE), jnp.float32)
    return pl.pallas_call(
        kernel,
        out_shape=(out, out),
        in_specs=[vmem, vmem],
        out_specs=(vmem, vmem),
        scratch_shapes=[
            pltpu.VMEM((STEPS, 4 * CH, 4 * KX), jnp.bfloat16),
            pltpu.VMEM((2, 4, SUB, 4 * KX), jnp.bfloat16),
            pltpu.VMEM((STEPS, 4, 2, CH, WIDE), jnp.float32),
            pltpu.VMEM((STEPS, 2, 4, CH, WIDE), jnp.int16),
            pltpu.VMEM((STEPS, 2, 4, CH, WIDE), jnp.int16),
            pltpu.VMEM((STEPS, CH, WIDE), jnp.int16),
            pltpu.VMEM((4, STEPS, CH, PIECE), jnp.int16),
            pltpu.VMEM((4, STEPS, CH, PIECE), jnp.int16),
            pltpu.VMEM((STEPS, 4, CH, PIECE), jnp.int16),
            pltpu.VMEM((STEPS, 4, CH, PIECE), jnp.int16),
            pltpu.SemaphoreType.DMA((COPIES,)),
            pltpu.SemaphoreType.DMA((COPIES,)),
            pltpu.SemaphoreType.DMA((4 * STEPS,)),
        ],
        compiler_params=pltpu.CompilerParams(
            collective_id=0, has_side_effects=True, vmem_limit_bytes=48 * 1024 * 1024),
        cost_estimate=pl.CostEstimate(
            flops=2 * 640 * 1280 * 2048, bytes_accessed=4 * 1024 * 1024, transcendentals=0),
    )(slabs, gammas)


def on_device(slabs, gammas, occupied, energies):
    block = slabs.shape[0]
    sub = block // 4

    row, col, aux = lax.axis_index("row"), lax.axis_index("col"), lax.axis_index("aux")
    s = slabs.reshape(4, STEPS, sub // STEPS, KX).transpose(1, 0, 2, 3)
    s = jnp.pad(s, ((0, 0), (0, 0), (0, CH - sub // STEPS), (0, 0))).reshape(STEPS, 4 * CH, KX)
    g = jnp.pad(gammas.reshape(4, sub, KX), ((0, 0), (0, SUB - sub), (0, 0)))
    direct, mirror = exchange(s, g)
    own = direct[:, :, :LAST, :sub].transpose(1, 2, 0, 3).reshape(sub, block)
    other = mirror[:, :, :LAST, :sub].reshape(block, sub).T
    gradient = 2.0 * (own - other)
    row_start = row * block + aux * sub
    col_start = col * block
    energy_rows = lax.dynamic_slice_in_dim(energies, row_start, sub)
    energy_cols = lax.dynamic_slice_in_dim(energies, col_start, block)
    occ_rows = lax.dynamic_slice_in_dim(occupied, row_start, sub)
    occ_cols = lax.dynamic_slice_in_dim(occupied, col_start, block)
    nonredundant = occ_rows[:, None] + occ_cols[None, :] - 2 * occ_rows[:, None] * occ_cols[None, :]
    denominator = 4.0 * jnp.abs(energy_rows[:, None] - energy_cols[None, :]) + 0.5
    rotation_step = -nonredundant.astype(jnp.float32) * gradient / denominator
    return (gradient, rotation_step)


def solution(mesh):
    placed = (P("row", "col", "aux"), P("row", "col", "aux"), P(), P())
    return jax.shard_map(
        on_device,
        mesh=mesh,
        in_specs=placed,
        out_specs=(P(("row", "aux"), "col"), P(("row", "aux"), "col")),
        check_vma=False,
    )
```

```python
import jax
import jax.numpy as jnp
from jax import lax
from jax.experimental import pallas as pl
from jax.experimental.pallas import tpu as pltpu
from jax.sharding import PartitionSpec as P

SUB = 160
ROWS = (96, 64)
FIRST = (0, ROWS[0])
LANES = 128
REST = SUB - LANES
WIDE = 4 * SUB
KX = 512
FOLD = tuple(-(-r // 32) * 8 for r in ROWS)
PACKED = tuple(r + -(-f // 16) * 16 for r, f in zip(ROWS, FOLD))
TOP = 32760.0
FINE = 128.0
PLACE = (0, 1, 3, 2)
GROUPS = ((0, 0, 3 * LANES, 1), (0, 3 * LANES, WIDE, 1), (1, 0, WIDE, 0))
MESH = pl.DeviceIdType.MESH


def encode(v):
    last = v.shape[0] - 1
    inside = lax.broadcasted_iota(jnp.int32, v.shape, 0) < last
    size = jnp.where(inside, jnp.abs(v), 0.0)
    largest = jnp.maximum(jnp.max(size, axis=0, keepdims=True), 1e-30)
    scale = jnp.ceil(jnp.log2(largest) * FINE)
    code = (jnp.sqrt(size) * (jnp.exp2(scale * (-0.5 / FINE)) * TOP) + 0.5).astype(jnp.int32)
    code = jnp.where(v < 0.0, -code, code)
    return jnp.where(inside, code, scale.astype(jnp.int32)).astype(jnp.int16)


def decode(code):
    value = code.astype(jnp.int32).astype(jnp.float32)
    root = value * (jnp.exp2(value[value.shape[0] - 1:] * (0.5 / FINE)) * (1.0 / TOP))
    return root * jnp.abs(root)


def fold(rest, t, h):
    size = FOLD[h]
    lane = lax.broadcasted_iota(jnp.int32, (size, LANES), 1)
    out = jnp.zeros((size, LANES), jnp.int32)
    for g in range(4):
        rows = rest[size * g:min(size * (g + 1), ROWS[h])]
        if rows.shape[0] < size:
            rows = jnp.concatenate([rows, jnp.zeros((size - rows.shape[0], LANES), jnp.int32)], axis=0)
        if g != t:
            rows = pltpu.roll(rows, (REST * (g - t)) % LANES, 1)
        out = jnp.where(lane // REST == g, rows, out)
    more = PACKED[h] - ROWS[h] - size
    return jnp.concatenate([out, jnp.zeros((more, LANES), jnp.int32)], axis=0) if more else out


def unfold(codes, h):
    parts = []
    for g in range(4):
        rows = codes[:min(FOLD[h], ROWS[h] - FOLD[h] * g)]
        parts.append(pltpu.roll(rows, LANES - REST * g, 1) if g else rows)
    return jnp.concatenate(parts, axis=0)


def kernel(s_ref, g_ref, direct, mirror, sbuf, gbuf, fock, *rest):
    n = len(GROUPS)
    outgoing, incoming, rest = rest[:n], rest[n:2 * n], rest[2 * n:]
    reduced, packed, direct_codes, mirror_codes, by_y, by_x = (rest[2 * i:2 * i + 2] for i in range(6))
    send, recv, loc = rest[12:]

    row, col, aux = lax.axis_index("row"), lax.axis_index("col"), lax.axis_index("aux")
    y, c = row // 2, row % 2
    x, zlo = col // 2, col % 2
    z = 2 * aux + zlo

    def at(row_=row, col_=col, aux_=aux):
        return {"row": row_, "col": col_, "aux": aux_}

    def x_at(d):
        return at(col_=2 * ((x + d) % 4) + zlo)

    def y_at(d):
        return at(row_=2 * ((y + d) % 4) + c)

    def z_at(d):
        there = (z + d) % 8
        return at(col_=2 * x + there % 2, aux_=there // 2)

    def swapped(m):
        return at(2 * y + zlo, 2 * x + c, m)

    other = at(row_=2 * y + (1 - c))
    same_core = zlo == c

    barrier = pltpu.get_barrier_semaphore()

    def greet(dev):
        pl.semaphore_signal(barrier, inc=1, device_id=dev, device_id_type=MESH)

    for dev in (x_at(1), x_at(3), x_at(2), y_at(1), y_at(3), y_at(2), other, z_at(1), z_at(7)):
        greet(dev)
    for r in range(4):
        @pl.when(jnp.logical_not(jnp.logical_and(same_core, aux == r)))
        def _():
            greet(swapped(r))

    pl.semaphore_wait(barrier, 13 - same_core.astype(jnp.int32))

    sends = []
    count = [0]

    def slots(k):
        count[0] += k
        return list(range(count[0] - k, count[0]))

    def remote(n_send, n_recv, src, dst, dev):
        return pltpu.make_async_remote_copy(
            src_ref=src, dst_ref=dst, send_sem=send.at[n_send], recv_sem=recv.at[n_recv],
            device_id=dev, device_id_type=MESH)

    def put(n, src, dst, dev):
        copy = remote(n, n, src, dst, dev)
        copy.start()
        sends.append(copy)

    def got(n, dst, dev):
        remote(n, n, dst, dst, dev).wait_recv()

    lanes = [pl.ds(KX * p, KX) for p in range(4)]

    a2a, cross = slots(4), [slots(4) for _ in range(4)]
    g_out = [slots(4) for _ in range(4)]

    def piece(core, d, p):
        return gbuf.at[core, PLACE[d % 4], :, lanes[p]]

    def over(d, p):
        put(cross[d][p], piece(c, d, p), piece(c, d, p), other)

    def spread(p):
        for d in (1, 3):
            put(g_out[p][d], piece(c, 0, p), piece(c, 4 - d, p), y_at(d))
        over(0, p)

    def arrived(d):
        p = (4 - d) % 4
        got(a2a[d], piece(c, 0, p), x_at(4 - d))
        spread(p)

    def relay(p):
        for d in (3, 1):
            here = piece(c, d, p)
            got(g_out[p][4 - d], here, y_at(d))
            if d == (3 if p in (0, 1) else 1):
                put(g_out[p][2], here, piece(c, 2, p), y_at(4 - d))
            over(d, p)

    def relay_far(p):
        got(g_out[p][2], piece(c, 2, p), y_at(3 if p in (0, 1) else 1))
        over(2, p)

    def crossed(d):
        for p in range(4):
            got(cross[d][p], piece(1 - c, d, p), other)

    s_out = [slots(5) for _ in ROWS]

    def chunk_rows(h):
        return pl.ds(4 * FIRST[h], 4 * ROWS[h])

    def half_rows(h, i):
        return pl.ds(4 * FIRST[h] + 2 * ROWS[h] * i, 2 * ROWS[h])

    def send_rows(h):
        for d in (1, 3):
            put(s_out[h][d], s_ref.at[chunk_rows(h)], sbuf.at[chunk_rows(h), lanes[4 - d]], x_at(d))

    def forward_rows(h):
        for i, d in enumerate((1, 3)):
            got(s_out[h][d], sbuf.at[chunk_rows(h), lanes[4 - d]], x_at(4 - d))
            put(s_out[h][2 * i + 2], sbuf.at[half_rows(h, i), lanes[4 - d]],
                sbuf.at[half_rows(h, i), lanes[2]], x_at(d))

    def finish_rows(h):
        for i, d in enumerate((1, 3)):
            got(s_out[h][2 * i + 2], sbuf.at[half_rows(h, i), lanes[2]], x_at(4 - d))

    def multiply(h, core, near, far):
        a = sbuf[4 * FIRST[h]:4 * (FIRST[h] + ROWS[h])]

        def block(b, first, size):
            out = lax.dot_general(a, b, (((1,), (1,)), ((), ())), preferred_element_type=jnp.float32)
            fock[:, core, FIRST[h]:FIRST[h] + ROWS[h], first:first + size] = out.reshape(4, ROWS[h], size)

        if near and far:
            block(gbuf[core, :, 0:LANES].reshape(4 * LANES, 4 * KX), 0, 4 * LANES)
        elif near:
            block(gbuf[core, 0:3, 0:LANES].reshape(3 * LANES, 4 * KX), 0, 3 * LANES)
        elif far:
            block(gbuf[core, 3, 0:LANES], 3 * LANES, LANES)
        if far:
            block(gbuf[core, :, LANES:SUB].reshape(4 * REST, 4 * KX), 4 * LANES, 4 * REST)

    rs = [[slots(4 if way == longer else 3) for way in range(2)] for _, _, _, longer in GROUPS]

    def sums(k, d, i):
        h, first, _, _ = GROUPS[k]
        there = (z + d) % 8
        return there // 2, there % 2, pl.ds(FIRST[h], ROWS[h]), pl.ds(first + LANES * i, LANES)

    def tiles(k):
        return range((GROUPS[k][2] - GROUPS[k][1]) // LANES)

    def hop(k, step):
        for way in range(2):
            hops = len(rs[k][way])
            if step >= hops:
                continue
            sign = 1 if way == 0 else 7
            if step > 0:
                got(rs[k][way][step - 1], incoming[k].at[way, step - 1], z_at(8 - sign))
            for i in tiles(k):
                cols = pl.ds(LANES * i, LANES)
                v = fock[sums(k, sign * (hops - step), i)]
                if step > 0:
                    v += decode(incoming[k][way, step - 1, :, cols])
                outgoing[k][way, step, :, cols] = encode(v)
            put(rs[k][way][step], outgoing[k].at[way, step], incoming[k].at[way, step], z_at(sign))

    def own(k):
        h, first, _, _ = GROUPS[k]
        for way in range(2):
            hops = len(rs[k][way])
            got(rs[k][way][-1], incoming[k].at[way, hops - 1], z_at(7 if way == 0 else 1))
        for i in tiles(k):
            v = fock[sums(k, 0, i)]
            for way in range(2):
                v += decode(incoming[k][way, len(rs[k][way]) - 1, :, pl.ds(LANES * i, LANES)])
            reduced[h][:, first + LANES * i:first + LANES * (i + 1)] = encode(v)

    x_out, y_out = [slots(4) for _ in ROWS], [slots(4) for _ in ROWS]
    t_out, m_out = [slots(4) for _ in ROWS], [slots(4) for _ in ROWS]

    def local(n, src, dst):
        return pltpu.make_async_copy(src, dst, loc.at[n])

    def leave(h):
        shared = reduced[h][:, 4 * LANES:].astype(jnp.int32)
        for d in (2, 1, 3, 0):
            t = PLACE[d]
            packed[h][d, 0:ROWS[h]] = reduced[h][:, LANES * t:LANES * (t + 1)]
            packed[h][d, ROWS[h]:PACKED[h]] = fold(shared, t, h).astype(jnp.int16)
            if d:
                put(y_out[h][d], packed[h].at[d], by_y[h].at[y], y_at(d))
        for d in (2, 1, 3):
            put(x_out[h][d], packed[h].at[(x + d - y + 4) % 4], direct_codes[h].at[x], x_at(d))
        copies = (local(4 * h, packed[h].at[0], by_y[h].at[y]),
                  local(4 * h + 1, packed[h].at[(x - y + 4) % 4], direct_codes[h].at[x]))
        for copy in copies:
            copy.start()
        for copy in copies:
            copy.wait()

    def along_x(h, d):
        t = (y + d) % 4
        return remote(t_out[h][d], t_out[h][0] + x, by_y[h].at[t], by_x[h].at[x], at(col_=2 * t + zlo))

    def along_z(h, m):
        return remote(m_out[h][m], m_out[h][0] + aux, by_x[h].at[m], mirror_codes[h].at[aux], swapped(m))

    def turn(h):
        for d in (0, 1, 3, 2):
            t = (y + d) % 4
            if d:
                got(y_out[h][4 - d], by_y[h].at[t], y_at(d))

            @pl.when(t == x)
            def _():
                copy = local(4 * h + 2, by_y[h].at[t], by_x[h].at[x])
                copy.start()
                copy.wait()

            @pl.when(t != x)
            def _():
                along_x(h, d).start()

    def swap(h):
        for m in range(4):
            @pl.when(m != x)
            def _():
                got(t_out[h][m], by_x[h].at[m], at(col_=2 * m + zlo))

            here = jnp.logical_and(same_core, aux == m)

            @pl.when(here)
            def _():
                copy = local(4 * h + 3, by_x[h].at[m], mirror_codes[h].at[aux])
                copy.start()
                copy.wait()

            @pl.when(jnp.logical_not(here))
            def _():
                along_z(h, m).start()

    def arrive(h):
        for d in (1, 2, 3):
            got(x_out[h][d], direct_codes[h].at[(x + 4 - d) % 4], x_at(4 - d))
        for r in range(4):
            @pl.when(jnp.logical_not(jnp.logical_and(same_core, aux == r)))
            def _():
                got(m_out[h][r], mirror_codes[h].at[r], swapped(r))

    def unpack(h):
        def one(i, carry):
            for codes, out in ((direct_codes[h], direct), (mirror_codes[h], mirror)):
                main, shared = codes[i, 0:ROWS[h]], codes[i, ROWS[h]:PACKED[h]].astype(jnp.int32)
                rows = slice(FIRST[h], FIRST[h] + ROWS[h])
                out[i, rows, 0:LANES] = decode(main)
                out[i, rows, LANES:2 * LANES] = decode(unfold(shared, h))
            return carry

        lax.fori_loop(0, 4, one, 0)

    for d in (1, 3, 2):
        put(a2a[d], g_ref.at[(x + d) % 4], piece(c, 0, 4 - d), x_at(d))
    gbuf[c, 0, :, 0:KX] = g_ref[x]
    spread(0)
    sbuf[:, 0:KX] = s_ref[...]
    arrived(1)
    arrived(3)
    send_rows(0)
    relay(0)
    arrived(2)
    relay(3)
    relay(1)
    forward_rows(0)
    send_rows(1)
    relay(2)
    for d in (0, 1, 3):
        crossed(d)
    finish_rows(0)
    multiply(0, c, True, False)
    multiply(0, 1 - c, True, False)
    hop(0, 0)
    for p in (0, 3, 1, 2):
        relay_far(p)
    multiply(0, c, False, True)
    forward_rows(1)
    hop(0, 1)
    crossed(2)
    multiply(0, 1 - c, False, True)
    hop(1, 0)
    hop(0, 2)
    finish_rows(1)
    multiply(1, c, True, True)
    multiply(1, 1 - c, True, True)
    hop(2, 0)
    hop(1, 1)
    hop(0, 3)
    hop(2, 1)
    hop(1, 2)
    own(0)
    hop(2, 2)
    hop(1, 3)
    own(1)
    leave(0)
    hop(2, 3)
    turn(0)
    own(2)
    leave(1)
    swap(0)
    turn(1)
    swap(1)
    arrive(0)
    unpack(0)
    arrive(1)
    unpack(1)
    for copy in sends:
        copy.wait_send()
    for h in range(2):
        for d in range(4):
            @pl.when((y + d) % 4 != x)
            def _():
                along_x(h, d).wait_send()
        for m in range(4):
            @pl.when(jnp.logical_not(jnp.logical_and(same_core, aux == m)))
            def _():
                along_z(h, m).wait_send()


COPIES = 4 + 16 + 16 + 10 + 7 * len(GROUPS) + 32


def exchange(slabs, gammas):
    vmem = pl.BlockSpec(memory_space=pltpu.VMEM)
    out = jax.ShapeDtypeStruct((4, SUB, 2 * LANES), jnp.float32)
    hops = [pltpu.VMEM((2, 4, ROWS[h], last - first), jnp.int16) for h, first, last, _ in GROUPS]
    pieces = [pltpu.VMEM((4, p, LANES), jnp.int16) for p in PACKED]
    return pl.pallas_call(
        kernel,
        out_shape=(out, out),
        in_specs=[vmem, vmem],
        out_specs=(vmem, vmem),
        scratch_shapes=[
            pltpu.VMEM((4 * SUB, 4 * KX), jnp.bfloat16),
            pltpu.VMEM((2, 4, SUB, 4 * KX), jnp.bfloat16),
            pltpu.VMEM((4, 2, SUB, WIDE), jnp.float32),
            *hops, *hops,
            *[pltpu.VMEM((r, WIDE), jnp.int16) for r in ROWS],
            *pieces, *pieces, *pieces, *pieces, *pieces,
            pltpu.SemaphoreType.DMA((COPIES,)),
            pltpu.SemaphoreType.DMA((COPIES,)),
            pltpu.SemaphoreType.DMA((8,)),
        ],
        compiler_params=pltpu.CompilerParams(
            collective_id=0, has_side_effects=True, vmem_limit_bytes=48 * 1024 * 1024),
        cost_estimate=pl.CostEstimate(
            flops=2 * 640 * 1280 * 2048, bytes_accessed=4 * 1024 * 1024, transcendentals=0),
    )(slabs, gammas)


def on_device(slabs, gammas, occupied, energies):
    block = slabs.shape[0]
    sub = block // 4
    row, col, aux = lax.axis_index("row"), lax.axis_index("col"), lax.axis_index("aux")
    split = ROWS[0] - 1
    rows = slabs.reshape(4, sub, KX)
    parts = [jnp.pad(part, ((0, 0), (0, 1), (0, 0))).reshape(-1, KX) for part in (rows[:, :split], rows[:, split:])]
    g = jnp.pad(gammas.reshape(4, sub, KX), ((0, 0), (0, SUB - sub), (0, 0)))
    direct, mirror = exchange(jnp.concatenate(parts), g)

    def trim(a):
        return jnp.concatenate([a[:, :split, :sub], a[:, split + 1:SUB - 1, :sub]], axis=1)

    own = trim(direct).transpose(1, 0, 2).reshape(sub, block)
    other = trim(mirror).reshape(block, sub).T
    gradient = 2.0 * (own - other)
    row_start = row * block + aux * sub
    col_start = col * block
    energy_rows = lax.dynamic_slice_in_dim(energies, row_start, sub)
    energy_cols = lax.dynamic_slice_in_dim(energies, col_start, block)
    occ_rows = lax.dynamic_slice_in_dim(occupied, row_start, sub)
    occ_cols = lax.dynamic_slice_in_dim(occupied, col_start, block)
    nonredundant = occ_rows[:, None] + occ_cols[None, :] - 2 * occ_rows[:, None] * occ_cols[None, :]
    denominator = 4.0 * jnp.abs(energy_rows[:, None] - energy_cols[None, :]) + 0.5
    rotation_step = -nonredundant.astype(jnp.float32) * gradient / denominator
    return (gradient, rotation_step)


def solution(mesh):
    placed = (P("row", "col", "aux"), P("row", "col", "aux"), P(), P())
    return jax.shard_map(
        on_device,
        mesh=mesh,
        in_specs=placed,
        out_specs=(P(("row", "aux"), "col"), P(("row", "aux"), "col")),
        check_vma=False,
    )
```

```python
import jax
import jax.numpy as jnp
from jax import lax
from jax.experimental import pallas as pl
from jax.experimental.pallas import tpu as pltpu
from jax.sharding import PartitionSpec as P

SUB = 160
ROWS = (96, 64)
FIRST = (0, ROWS[0])
LANES = 128
REST = SUB - LANES
WIDE = 4 * SUB
KX = 512
FOLD = tuple(-(-r // 32) * 8 for r in ROWS)
PACKED = tuple(r + -(-f // 16) * 16 for r, f in zip(ROWS, FOLD))
TOP = 32760.0
FINE = 128.0
PLACE = (0, 1, 3, 2)
GROUPS = ((0, 0, 3 * LANES, 1), (0, 3 * LANES, WIDE, 1), (1, 0, WIDE, 0))
MESH = pl.DeviceIdType.MESH


def encode(v):
    last = v.shape[0] - 1
    inside = lax.broadcasted_iota(jnp.int32, v.shape, 0) < last
    size = jnp.where(inside, jnp.abs(v), 0.0)
    largest = jnp.maximum(jnp.max(size, axis=0, keepdims=True), 1e-30)
    scale = jnp.ceil(jnp.log2(largest) * FINE)
    code = (jnp.sqrt(size) * (jnp.exp2(scale * (-0.5 / FINE)) * TOP) + 0.5).astype(jnp.int32)
    code = jnp.where(v < 0.0, -code, code)
    return jnp.where(inside, code, scale.astype(jnp.int32)).astype(jnp.int16)


def decode(code):
    value = code.astype(jnp.int32).astype(jnp.float32)
    root = value * (jnp.exp2(value[value.shape[0] - 1:] * (0.5 / FINE)) * (1.0 / TOP))
    return root * jnp.abs(root)


def fold(rest, t, h):
    size = FOLD[h]
    lane = lax.broadcasted_iota(jnp.int32, (size, LANES), 1)
    out = jnp.zeros((size, LANES), jnp.int32)
    for g in range(4):
        rows = rest[size * g:min(size * (g + 1), ROWS[h])]
        if rows.shape[0] < size:
            rows = jnp.concatenate([rows, jnp.zeros((size - rows.shape[0], LANES), jnp.int32)], axis=0)
        if g != t:
            rows = pltpu.roll(rows, (REST * (g - t)) % LANES, 1)
        out = jnp.where(lane // REST == g, rows, out)
    more = PACKED[h] - ROWS[h] - size
    return jnp.concatenate([out, jnp.zeros((more, LANES), jnp.int32)], axis=0) if more else out


def unfold(codes, h):
    parts = []
    for g in range(4):
        rows = codes[:min(FOLD[h], ROWS[h] - FOLD[h] * g)]
        parts.append(pltpu.roll(rows, LANES - REST * g, 1) if g else rows)
    return jnp.concatenate(parts, axis=0)


def kernel(s_raw, g_raw, levels, gradient, rotation, direct, mirror, weight, g_ref, sbuf, gbuf, fock, *rest):
    n = len(GROUPS)
    outgoing, incoming, rest = rest[:n], rest[n:2 * n], rest[2 * n:]
    reduced, packed, direct_codes, mirror_codes, by_y, by_x = (rest[2 * i:2 * i + 2] for i in range(6))
    send, recv, loc = rest[12:]

    row, col, aux = lax.axis_index("row"), lax.axis_index("col"), lax.axis_index("aux")
    y, c = row // 2, row % 2
    x, zlo = col // 2, col % 2
    z = 2 * aux + zlo

    def at(row_=row, col_=col, aux_=aux):
        return {"row": row_, "col": col_, "aux": aux_}

    def x_at(d):
        return at(col_=2 * ((x + d) % 4) + zlo)

    def y_at(d):
        return at(row_=2 * ((y + d) % 4) + c)

    def z_at(d):
        there = (z + d) % 8
        return at(col_=2 * x + there % 2, aux_=there // 2)

    def swapped(m):
        return at(2 * y + zlo, 2 * x + c, m)

    other = at(row_=2 * y + (1 - c))
    same_core = zlo == c

    barrier = pltpu.get_barrier_semaphore()

    def greet(dev):
        pl.semaphore_signal(barrier, inc=1, device_id=dev, device_id_type=MESH)

    for dev in (x_at(1), x_at(3), x_at(2), y_at(1), y_at(3), y_at(2), other, z_at(1), z_at(7)):
        greet(dev)
    for r in range(4):
        @pl.when(jnp.logical_not(jnp.logical_and(same_core, aux == r)))
        def _():
            greet(swapped(r))

    pl.semaphore_wait(barrier, 13 - same_core.astype(jnp.int32))

    sends = []
    count = [0]

    def slots(k):
        count[0] += k
        return list(range(count[0] - k, count[0]))

    def remote(n_send, n_recv, src, dst, dev):
        return pltpu.make_async_remote_copy(
            src_ref=src, dst_ref=dst, send_sem=send.at[n_send], recv_sem=recv.at[n_recv],
            device_id=dev, device_id_type=MESH)

    def put(n, src, dst, dev):
        copy = remote(n, n, src, dst, dev)
        copy.start()
        sends.append(copy)

    def got(n, dst, dev):
        remote(n, n, dst, dst, dev).wait_recv()

    lanes = [pl.ds(KX * p, KX) for p in range(4)]

    a2a, cross = slots(4), [slots(4) for _ in range(4)]
    g_out = [slots(4) for _ in range(4)]

    def piece(core, d, p):
        return gbuf.at[core, PLACE[d % 4], :, lanes[p]]

    def over(d, p):
        put(cross[d][p], piece(c, d, p), piece(c, d, p), other)

    def spread(p):
        for d in (1, 3):
            put(g_out[p][d], piece(c, 0, p), piece(c, 4 - d, p), y_at(d))
        over(0, p)

    def arrived(d):
        p = (4 - d) % 4
        got(a2a[d], piece(c, 0, p), x_at(4 - d))
        spread(p)

    def relay(p):
        for d in (3, 1):
            here = piece(c, d, p)
            got(g_out[p][4 - d], here, y_at(d))
            if d == (3 if p in (0, 1) else 1):
                put(g_out[p][2], here, piece(c, 2, p), y_at(4 - d))
            over(d, p)

    def relay_far(p):
        got(g_out[p][2], piece(c, 2, p), y_at(3 if p in (0, 1) else 1))
        over(2, p)

    def crossed(d):
        for p in range(4):
            got(cross[d][p], piece(1 - c, d, p), other)

    s_out, s_far = [slots(4) for _ in ROWS], [slots(2) for _ in ROWS]

    def half_rows(h, i):
        return pl.ds(4 * FIRST[h] + 2 * ROWS[h] * i, 2 * ROWS[h])

    def send_rows(h):
        for part in range(2):
            for i, d in enumerate((1, 3)):
                rows = half_rows(h, (i + part) % 2)
                put(s_out[h][2 * i + part], sbuf.at[rows, lanes[0]], sbuf.at[rows, lanes[4 - d]], x_at(d))

    def near_rows(h, part):
        for i, d in enumerate((1, 3)):
            rows = half_rows(h, (i + part) % 2)
            got(s_out[h][2 * i + part], sbuf.at[rows, lanes[4 - d]], x_at(4 - d))
            if part == 0:
                put(s_far[h][i], sbuf.at[rows, lanes[4 - d]], sbuf.at[rows, lanes[2]], x_at(d))

    def forward_rows(h):
        near_rows(h, 0)

    def finish_rows(h):
        near_rows(h, 1)
        for i, d in enumerate((1, 3)):
            got(s_far[h][i], sbuf.at[half_rows(h, i), lanes[2]], x_at(4 - d))

    def multiply(h, core, near, far):
        a = sbuf[4 * FIRST[h]:4 * (FIRST[h] + ROWS[h])]

        def block(b, first, size):
            out = lax.dot_general(a, b, (((1,), (1,)), ((), ())), preferred_element_type=jnp.float32)
            fock[:, core, FIRST[h]:FIRST[h] + ROWS[h], first:first + size] = out.reshape(4, ROWS[h], size)

        if near and far:
            block(gbuf[core, :, 0:LANES].reshape(4 * LANES, 4 * KX), 0, 4 * LANES)
        elif near:
            block(gbuf[core, 0:3, 0:LANES].reshape(3 * LANES, 4 * KX), 0, 3 * LANES)
        elif far:
            block(gbuf[core, 3, 0:LANES], 3 * LANES, LANES)
        if far:
            block(gbuf[core, :, LANES:SUB].reshape(4 * REST, 4 * KX), 4 * LANES, 4 * REST)

    rs = [[slots(4 if way == longer else 3) for way in range(2)] for _, _, _, longer in GROUPS]

    def sums(k, d, i):
        h, first, _, _ = GROUPS[k]
        there = (z + d) % 8
        return there // 2, there % 2, pl.ds(FIRST[h], ROWS[h]), pl.ds(first + LANES * i, LANES)

    def tiles(k):
        return range((GROUPS[k][2] - GROUPS[k][1]) // LANES)

    def hop(k, step):
        for way in range(2):
            hops = len(rs[k][way])
            if step >= hops:
                continue
            sign = 1 if way == 0 else 7
            if step > 0:
                got(rs[k][way][step - 1], incoming[k].at[way, step - 1], z_at(8 - sign))
            for i in tiles(k):
                cols = pl.ds(LANES * i, LANES)
                v = fock[sums(k, sign * (hops - step), i)]
                if step > 0:
                    v += decode(incoming[k][way, step - 1, :, cols])
                outgoing[k][way, step, :, cols] = encode(v)
            put(rs[k][way][step], outgoing[k].at[way, step], incoming[k].at[way, step], z_at(sign))

    def own(k):
        h, first, _, _ = GROUPS[k]
        for way in range(2):
            hops = len(rs[k][way])
            got(rs[k][way][-1], incoming[k].at[way, hops - 1], z_at(7 if way == 0 else 1))
        for i in tiles(k):
            v = fock[sums(k, 0, i)]
            for way in range(2):
                v += decode(incoming[k][way, len(rs[k][way]) - 1, :, pl.ds(LANES * i, LANES)])
            reduced[h][:, first + LANES * i:first + LANES * (i + 1)] = encode(v)

    x_out, y_out = [slots(4) for _ in ROWS], [slots(4) for _ in ROWS]
    t_out, m_out = [slots(4) for _ in ROWS], [slots(4) for _ in ROWS]

    def local(n, src, dst):
        return pltpu.make_async_copy(src, dst, loc.at[n])

    def leave(h):
        shared = reduced[h][:, 4 * LANES:].astype(jnp.int32)
        for d in (2, 1, 3, 0):
            t = PLACE[d]
            packed[h][d, 0:ROWS[h]] = reduced[h][:, LANES * t:LANES * (t + 1)]
            packed[h][d, ROWS[h]:PACKED[h]] = fold(shared, t, h).astype(jnp.int16)
            if d:
                put(y_out[h][d], packed[h].at[d], by_y[h].at[y], y_at(d))
        for d in (2, 1, 3):
            put(x_out[h][d], packed[h].at[(x + d - y + 4) % 4], direct_codes[h].at[x], x_at(d))
        copies = (local(4 * h, packed[h].at[0], by_y[h].at[y]),
                  local(4 * h + 1, packed[h].at[(x - y + 4) % 4], direct_codes[h].at[x]))
        for copy in copies:
            copy.start()
        for copy in copies:
            copy.wait()

    def along_x(h, d):
        t = (y + d) % 4
        return remote(t_out[h][d], t_out[h][0] + x, by_y[h].at[t], by_x[h].at[x], at(col_=2 * t + zlo))

    def along_z(h, m):
        return remote(m_out[h][m], m_out[h][0] + aux, by_x[h].at[m], mirror_codes[h].at[aux], swapped(m))

    def turn(h):
        for d in (0, 1, 3, 2):
            t = (y + d) % 4
            if d:
                got(y_out[h][4 - d], by_y[h].at[t], y_at(d))

            @pl.when(t == x)
            def _():
                copy = local(4 * h + 2, by_y[h].at[t], by_x[h].at[x])
                copy.start()
                copy.wait()

            @pl.when(t != x)
            def _():
                along_x(h, d).start()

    def swap(h):
        for m in range(4):
            @pl.when(m != x)
            def _():
                got(t_out[h][m], by_x[h].at[m], at(col_=2 * m + zlo))

            here = jnp.logical_and(same_core, aux == m)

            @pl.when(here)
            def _():
                copy = local(4 * h + 3, by_x[h].at[m], mirror_codes[h].at[aux])
                copy.start()
                copy.wait()

            @pl.when(jnp.logical_not(here))
            def _():
                along_z(h, m).start()

    def arrive(h):
        for d in (1, 2, 3):
            got(x_out[h][d], direct_codes[h].at[(x + 4 - d) % 4], x_at(4 - d))
        for r in range(4):
            @pl.when(jnp.logical_not(jnp.logical_and(same_core, aux == r)))
            def _():
                got(m_out[h][r], mirror_codes[h].at[r], swapped(r))

    def unpack(h):
        def one(i, carry):
            for codes, out in ((direct_codes[h], direct), (mirror_codes[h], mirror)):
                main, shared = codes[i, 0:ROWS[h]], codes[i, ROWS[h]:PACKED[h]].astype(jnp.int32)
                rows = slice(FIRST[h], FIRST[h] + ROWS[h])
                out[i, rows, 0:LANES] = decode(main)
                out[i, rows, LANES:2 * LANES] = decode(unfold(shared, h))
            return carry

        lax.fori_loop(0, 4, one, 0)

    def flat(ref, first, rows):
        return ref[first:first + rows].reshape(rows, KX)

    block = s_raw.shape[0] // 4
    for m in range(4):
        g_ref[m, SUB - 16:SUB] = jnp.zeros((16, KX), jnp.bfloat16)
        g_ref[m, 0:block] = flat(g_raw, block * m, block)
    def window(first, size):
        wide = LANES * (size // LANES + 2)
        base = pl.multiple_of(first // LANES * LANES, LANES)
        return pltpu.roll(levels[:, pl.ds(base, wide)], (wide - first % LANES) % wide, 1)

    def weigh():
        n = 4 * block
        across = window(n * col, n)[:, :n]
        down = window(block * (4 * row + aux), block)[:, :2 * LANES].T[:block]
        occupied, filled = down[:, 1:2], across[1:2]
        pairs = occupied + filled - 2.0 * occupied * filled
        weight[...] = -pairs / (4.0 * jnp.abs(down[:, 0:1] - across[0:1]) + 0.5)

    def finish():
        lines = [slice(FIRST[h], FIRST[h] + min(ROWS[h] - 1, block - FIRST[h] + h)) for h in range(2)]
        mine = jnp.concatenate([direct[m, :, :block] for m in range(4)], axis=1)
        turned = [mirror[r].T[:block] for r in range(4)]
        theirs = jnp.concatenate([t[:, part] for t in turned for part in lines], axis=1)
        mine = jnp.concatenate([mine[part] for part in lines], axis=0)
        total = 2.0 * (mine - theirs)
        gradient[...] = total
        rotation[...] = weight[...] * total

    for d in (1, 3, 2):
        put(a2a[d], g_ref.at[(x + d) % 4], piece(c, 0, 4 - d), x_at(d))
    gbuf[c, 0, :, 0:KX] = g_ref[x]
    spread(0)
    for h in range(2):
        rows = min(ROWS[h] - 1, block - FIRST[h] + h)
        for r in range(4):
            first = 4 * FIRST[h] + ROWS[h] * r
            sbuf[first + ROWS[h] - 16:first + ROWS[h], 0:KX] = jnp.zeros((16, KX), jnp.bfloat16)
            sbuf[first:first + rows, 0:KX] = flat(s_raw, block * r + FIRST[h] - h, rows)
    arrived(1)
    arrived(3)
    send_rows(0)
    weigh()
    relay(0)
    arrived(2)
    relay(3)
    forward_rows(0)
    send_rows(1)
    relay(1)
    relay(2)
    for d in (0, 1, 3):
        crossed(d)
    finish_rows(0)
    multiply(0, c, True, False)
    multiply(0, 1 - c, True, False)
    hop(0, 0)
    for p in (0, 3, 1, 2):
        relay_far(p)
    multiply(0, c, False, True)
    forward_rows(1)
    hop(0, 1)
    crossed(2)
    multiply(0, 1 - c, False, True)
    hop(1, 0)
    hop(0, 2)
    finish_rows(1)
    multiply(1, c, True, True)
    multiply(1, 1 - c, True, True)
    hop(2, 0)
    hop(1, 1)
    hop(0, 3)
    hop(2, 1)
    hop(1, 2)
    own(0)
    hop(2, 2)
    hop(1, 3)
    hop(2, 3)
    own(1)
    leave(0)
    turn(0)
    own(2)
    leave(1)
    swap(0)
    turn(1)
    swap(1)
    arrive(0)
    unpack(0)
    arrive(1)
    unpack(1)
    finish()
    for copy in sends:
        copy.wait_send()
    for h in range(2):
        for d in range(4):
            @pl.when((y + d) % 4 != x)
            def _():
                along_x(h, d).wait_send()
        for m in range(4):
            @pl.when(jnp.logical_not(jnp.logical_and(same_core, aux == m)))
            def _():
                along_z(h, m).wait_send()


COPIES = 4 + 16 + 16 + 12 + 7 * len(GROUPS) + 32


def exchange(slabs, gammas, levels):
    vmem = pl.BlockSpec(memory_space=pltpu.VMEM)
    block = slabs.shape[0]
    out = jax.ShapeDtypeStruct((block // 4, block), jnp.float32)
    hops = [pltpu.VMEM((2, 4, ROWS[h], last - first), jnp.int16) for h, first, last, _ in GROUPS]
    pieces = [pltpu.VMEM((4, p, LANES), jnp.int16) for p in PACKED]
    return pl.pallas_call(
        kernel,
        out_shape=(out, out),
        in_specs=[vmem, vmem, vmem],
        out_specs=(vmem, vmem),
        scratch_shapes=[
            pltpu.VMEM((4, SUB, 2 * LANES), jnp.float32),
            pltpu.VMEM((4, SUB, 2 * LANES), jnp.float32),
            pltpu.VMEM((block // 4, block), jnp.float32),
            pltpu.VMEM((4, SUB, KX), jnp.bfloat16),
            pltpu.VMEM((4 * SUB, 4 * KX), jnp.bfloat16),
            pltpu.VMEM((2, 4, SUB, 4 * KX), jnp.bfloat16),
            pltpu.VMEM((4, 2, SUB, WIDE), jnp.float32),
            *hops, *hops,
            *[pltpu.VMEM((r, WIDE), jnp.int16) for r in ROWS],
            *pieces, *pieces, *pieces, *pieces, *pieces,
            pltpu.SemaphoreType.DMA((COPIES,)),
            pltpu.SemaphoreType.DMA((COPIES,)),
            pltpu.SemaphoreType.DMA((8,)),
        ],
        compiler_params=pltpu.CompilerParams(
            collective_id=0, has_side_effects=True, vmem_limit_bytes=48 * 1024 * 1024),
        cost_estimate=pl.CostEstimate(
            flops=2 * 640 * 1280 * 2048, bytes_accessed=4 * 1024 * 1024, transcendentals=0),
    )(slabs, gammas, levels)


def on_device(slabs, gammas, occupied, energies):
    rows = jnp.stack([energies, occupied.astype(jnp.float32)])
    tail = -rows.shape[1] % LANES + 2 * LANES
    return exchange(slabs, gammas, jnp.pad(rows, ((0, 6), (0, tail))))


def solution(mesh):
    placed = (P("row", "col", "aux"), P("row", "col", "aux"), P(), P())
    return jax.shard_map(
        on_device,
        mesh=mesh,
        in_specs=placed,
        out_specs=(P(("row", "aux"), "col"), P(("row", "aux"), "col")),
        check_vma=False,
    )
```

```python
import jax
import jax.numpy as jnp
from jax import lax
from jax.experimental import pallas as pl
from jax.experimental.pallas import tpu as pltpu
from jax.sharding import PartitionSpec as P

SUB = 160
ROWS = (96, 64)
FIRST = (0, ROWS[0])
LANES = 128
REST = SUB - LANES
WIDE = 4 * SUB
KX = 512
FOLD = tuple(-(-r // 32) * 8 for r in ROWS)
PACKED = tuple(r + -(-f // 16) * 16 for r, f in zip(ROWS, FOLD))
TOP = 32760.0
FINE = 128.0
PLACE = (0, 1, 3, 2)
GROUPS = ((0, 0, 3 * LANES, 1), (0, 3 * LANES, WIDE, 1), (1, 0, WIDE, 0))
SHORT = (1, 2)
MESH = pl.DeviceIdType.MESH


def encode(v):
    last = v.shape[0] - 1
    inside = lax.broadcasted_iota(jnp.int32, v.shape, 0) < last
    size = jnp.where(inside, jnp.abs(v), 0.0)
    largest = jnp.maximum(jnp.max(size, axis=0, keepdims=True), 1e-30)
    scale = jnp.ceil(jnp.log2(largest) * FINE)
    code = (jnp.sqrt(size) * (jnp.exp2(scale * (-0.5 / FINE)) * TOP) + 0.5).astype(jnp.int32)
    code = jnp.where(v < 0.0, -code, code)
    return jnp.where(inside, code, scale.astype(jnp.int32)).astype(jnp.int16)


def decode(code):
    value = code.astype(jnp.int32).astype(jnp.float32)
    root = value * (jnp.exp2(value[value.shape[0] - 1:] * (0.5 / FINE)) * (1.0 / TOP))
    return root * jnp.abs(root)


def fold(rest, t, h):
    size = FOLD[h]
    lane = lax.broadcasted_iota(jnp.int32, (size, LANES), 1)
    out = jnp.zeros((size, LANES), jnp.int32)
    for g in range(4):
        rows = rest[size * g:min(size * (g + 1), ROWS[h])]
        if rows.shape[0] < size:
            rows = jnp.concatenate([rows, jnp.zeros((size - rows.shape[0], LANES), jnp.int32)], axis=0)
        if g != t:
            rows = pltpu.roll(rows, (REST * (g - t)) % LANES, 1)
        out = jnp.where(lane // REST == g, rows, out)
    more = PACKED[h] - ROWS[h] - size
    return jnp.concatenate([out, jnp.zeros((more, LANES), jnp.int32)], axis=0) if more else out


def unfold(codes, h):
    parts = []
    for g in range(4):
        rows = codes[:min(FOLD[h], ROWS[h] - FOLD[h] * g)]
        parts.append(pltpu.roll(rows, LANES - REST * g, 1) if g else rows)
    return jnp.concatenate(parts, axis=0)


def kernel(s_hbm, g_hbm, energies, occupied, gradient, weight, levels, direct, mirror, s_raw, g_raw, g_ref, sbuf, gbuf, fock, *rest):
    n = len(GROUPS)
    outgoing, incoming, rest = rest[:n], rest[n:2 * n], rest[2 * n:]
    reduced, packed, direct_codes, mirror_codes, by_y, by_x = (rest[2 * i:2 * i + 2] for i in range(6))
    send, recv, loc = rest[12:]

    fetch = [pltpu.make_async_copy(src, dst, loc.at[8 + i])
             for i, (src, dst) in enumerate(((g_hbm, g_raw), (s_hbm, s_raw)))]
    for copy in fetch:
        copy.start()

    row, col, aux = lax.axis_index("row"), lax.axis_index("col"), lax.axis_index("aux")
    y, c = row // 2, row % 2
    x, zlo = col // 2, col % 2
    z = 2 * aux + zlo

    def at(row_=row, col_=col, aux_=aux):
        return {"row": row_, "col": col_, "aux": aux_}

    def x_at(d):
        return at(col_=2 * ((x + d) % 4) + zlo)

    def y_at(d):
        return at(row_=2 * ((y + d) % 4) + c)

    def z_at(d):
        there = (z + d) % 8
        return at(col_=2 * x + there % 2, aux_=there // 2)

    def swapped(m):
        return at(2 * y + zlo, 2 * x + c, m)

    other = at(row_=2 * y + (1 - c))
    same_core = zlo == c

    barrier = pltpu.get_barrier_semaphore()

    def greet(dev):
        pl.semaphore_signal(barrier, inc=1, device_id=dev, device_id_type=MESH)

    for dev in (x_at(1), x_at(3), x_at(2), y_at(1), y_at(3), y_at(2), other, z_at(1), z_at(7), z_at(2), z_at(6)):
        greet(dev)
    for r in range(4):
        @pl.when(jnp.logical_not(jnp.logical_and(same_core, aux == r)))
        def _():
            greet(swapped(r))

    sends = []
    count = [0]

    def slots(k):
        count[0] += k
        return list(range(count[0] - k, count[0]))

    def remote(n_send, n_recv, src, dst, dev):
        return pltpu.make_async_remote_copy(
            src_ref=src, dst_ref=dst, send_sem=send.at[n_send], recv_sem=recv.at[n_recv],
            device_id=dev, device_id_type=MESH)

    def put(n, src, dst, dev):
        copy = remote(n, n, src, dst, dev)
        copy.start()
        sends.append(copy)

    def got(n, dst, dev):
        remote(n, n, dst, dst, dev).wait_recv()

    lanes = [pl.ds(KX * p, KX) for p in range(4)]

    a2a, cross = slots(4), [slots(4) for _ in range(4)]
    g_out = [slots(4) for _ in range(4)]

    def piece(core, d, p):
        return gbuf.at[core, PLACE[d % 4], :, lanes[p]]

    def over(d, p):
        put(cross[d][p], piece(c, d, p), piece(c, d, p), other)

    def spread(p):
        for d in (1, 3):
            put(g_out[p][d], piece(c, 0, p), piece(c, 4 - d, p), y_at(d))
        over(0, p)

    def arrived(d):
        p = (4 - d) % 4
        got(a2a[d], piece(c, 0, p), x_at(4 - d))
        spread(p)

    def relay(p):
        for d in (3, 1):
            here = piece(c, d, p)
            got(g_out[p][4 - d], here, y_at(d))
            if d == (3 if p in (0, 1) else 1):
                put(g_out[p][2], here, piece(c, 2, p), y_at(4 - d))
            over(d, p)

    def relay_far(p):
        got(g_out[p][2], piece(c, 2, p), y_at(3 if p in (0, 1) else 1))
        over(2, p)

    def crossed(d):
        for p in range(4):
            got(cross[d][p], piece(1 - c, d, p), other)

    s_out, s_far = [slots(4) for _ in ROWS], [slots(2) for _ in ROWS]

    def half_rows(h, i):
        return pl.ds(4 * FIRST[h] + 2 * ROWS[h] * i, 2 * ROWS[h])

    def send_rows(h):
        for part in range(2):
            for i, d in enumerate((1, 3)):
                rows = half_rows(h, (i + part) % 2)
                put(s_out[h][2 * i + part], sbuf.at[rows, lanes[0]], sbuf.at[rows, lanes[4 - d]], x_at(d))

    def near_rows(h, part):
        for i, d in enumerate((1, 3)):
            rows = half_rows(h, (i + part) % 2)
            got(s_out[h][2 * i + part], sbuf.at[rows, lanes[4 - d]], x_at(4 - d))
            if part == 0:
                put(s_far[h][i], sbuf.at[rows, lanes[4 - d]], sbuf.at[rows, lanes[2]], x_at(d))

    def forward_rows(h):
        near_rows(h, 0)

    def finish_rows(h):
        near_rows(h, 1)
        for i, d in enumerate((1, 3)):
            got(s_far[h][i], sbuf.at[half_rows(h, i), lanes[2]], x_at(4 - d))

    def multiply(h, core, near, far):
        a = sbuf[4 * FIRST[h]:4 * (FIRST[h] + ROWS[h])]

        def block(b, first, size):
            out = lax.dot_general(a, b, (((1,), (1,)), ((), ())), preferred_element_type=jnp.float32)
            fock[:, core, FIRST[h]:FIRST[h] + ROWS[h], first:first + size] = out.reshape(4, ROWS[h], size)

        if near and far:
            block(gbuf[core, :, 0:LANES].reshape(4 * LANES, 4 * KX), 0, 4 * LANES)
        elif near:
            block(gbuf[core, 0:3, 0:LANES].reshape(3 * LANES, 4 * KX), 0, 3 * LANES)
        elif far:
            block(gbuf[core, 3, 0:LANES], 3 * LANES, LANES)
        if far:
            block(gbuf[core, :, LANES:SUB].reshape(4 * REST, 4 * KX), 4 * LANES, 4 * REST)

    rs = [[slots(4 if way == longer else 3) for way in range(2)] for _, _, _, longer in GROUPS]

    def sums(k, d, i):
        h, first, _, _ = GROUPS[k]
        there = (z + d) % 8
        return there // 2, there % 2, pl.ds(FIRST[h], ROWS[h]), pl.ds(first + LANES * i, LANES)

    def tiles(k):
        return range((GROUPS[k][2] - GROUPS[k][1]) // LANES)

    def hop(k, step):
        for way in range(2):
            hops = len(rs[k][way])
            if step >= hops:
                continue
            sign = 1 if way == 0 else 7
            if step > 0:
                got(rs[k][way][step - 1], incoming[k].at[way, step - 1], z_at(8 - sign))
            for i in tiles(k):
                cols = pl.ds(LANES * i, LANES)
                v = fock[sums(k, sign * (hops - step), i)]
                if step > 0:
                    v += decode(incoming[k][way, step - 1, :, cols])
                outgoing[k][way, step, :, cols] = encode(v)
            put(rs[k][way][step], outgoing[k].at[way, step], incoming[k].at[way, step], z_at(sign))

    AWAY = (3, 1, 2, 4)
    REACH = (1, 1, 2, 2)

    def message(k, way, n, others):
        sign = 1 if way == 0 else 7
        for i in tiles(k):
            cols = pl.ds(LANES * i, LANES)
            v = fock[sums(k, sign * AWAY[n], i)]
            for m in others:
                v += decode(incoming[k][way, m, :, cols])
            outgoing[k][way, n, :, cols] = encode(v)
        put(rs[k][way][n], outgoing[k].at[way, n], incoming[k].at[way, n], z_at(sign * REACH[n]))

    def came(k, way, n):
        sign = 1 if way == 0 else 7
        got(rs[k][way][n], incoming[k].at[way, n], z_at((8 - sign) * REACH[n]))

    def begin(k):
        for n in (3, 0, 1):
            for way in range(2):
                if n < len(rs[k][way]):
                    message(k, way, n, ())

    def meet(k):
        for way in (1, 0):
            others = (0, 3) if len(rs[k][way]) == 4 else (0,)
            for n in others:
                came(k, way, n)
            message(k, way, 2, others)

    def own(k):
        h, first, _, _ = GROUPS[k]
        last = [(1, 2) if k in SHORT else (len(rs[k][way]) - 1,) for way in range(2)]
        for way in range(2):
            for n in last[way]:
                if k in SHORT:
                    came(k, way, n)
                else:
                    got(rs[k][way][n], incoming[k].at[way, n], z_at(7 if way == 0 else 1))
        for i in tiles(k):
            v = fock[sums(k, 0, i)]
            for way in range(2):
                for n in last[way]:
                    v += decode(incoming[k][way, n, :, pl.ds(LANES * i, LANES)])
            reduced[h][:, first + LANES * i:first + LANES * (i + 1)] = encode(v)

    x_out, y_out = [slots(4) for _ in ROWS], [slots(4) for _ in ROWS]
    t_out, m_out = [slots(4) for _ in ROWS], [slots(4) for _ in ROWS]

    def local(n, src, dst):
        return pltpu.make_async_copy(src, dst, loc.at[n])

    def leave(h):
        shared = reduced[h][:, 4 * LANES:].astype(jnp.int32)
        for d in (2, 1, 3, 0):
            t = PLACE[d]
            packed[h][d, 0:ROWS[h]] = reduced[h][:, LANES * t:LANES * (t + 1)]
            packed[h][d, ROWS[h]:PACKED[h]] = fold(shared, t, h).astype(jnp.int16)
            if d:
                put(y_out[h][d], packed[h].at[d], by_y[h].at[y], y_at(d))
        for d in (2, 1, 3):
            put(x_out[h][d], packed[h].at[(x + d - y + 4) % 4], direct_codes[h].at[x], x_at(d))
        copies = (local(4 * h, packed[h].at[0], by_y[h].at[y]),
                  local(4 * h + 1, packed[h].at[(x - y + 4) % 4], direct_codes[h].at[x]))
        for copy in copies:
            copy.start()
        for copy in copies:
            copy.wait()

    def along_x(h, d):
        t = (y + d) % 4
        return remote(t_out[h][d], t_out[h][0] + x, by_y[h].at[t], by_x[h].at[x], at(col_=2 * t + zlo))

    def along_z(h, m):
        return remote(m_out[h][m], m_out[h][0] + aux, by_x[h].at[m], mirror_codes[h].at[aux], swapped(m))

    def turn(h):
        for d in (0, 1, 3, 2):
            t = (y + d) % 4
            if d:
                got(y_out[h][4 - d], by_y[h].at[t], y_at(d))

            @pl.when(t == x)
            def _():
                copy = local(4 * h + 2, by_y[h].at[t], by_x[h].at[x])
                copy.start()
                copy.wait()

            @pl.when(t != x)
            def _():
                along_x(h, d).start()

    def swap(h):
        for m in range(4):
            @pl.when(m != x)
            def _():
                got(t_out[h][m], by_x[h].at[m], at(col_=2 * m + zlo))

            here = jnp.logical_and(same_core, aux == m)

            @pl.when(here)
            def _():
                copy = local(4 * h + 3, by_x[h].at[m], mirror_codes[h].at[aux])
                copy.start()
                copy.wait()

            @pl.when(jnp.logical_not(here))
            def _():
                along_z(h, m).start()

    def arrive(h):
        for d in (1, 2, 3):
            got(x_out[h][d], direct_codes[h].at[(x + 4 - d) % 4], x_at(4 - d))
        for r in range(4):
            @pl.when(jnp.logical_not(jnp.logical_and(same_core, aux == r)))
            def _():
                got(m_out[h][r], mirror_codes[h].at[r], swapped(r))

    def unpack(h):
        def one(i, carry):
            for codes, out in ((direct_codes[h], direct), (mirror_codes[h], mirror)):
                main, shared = codes[i, 0:ROWS[h]], codes[i, ROWS[h]:PACKED[h]].astype(jnp.int32)
                rows = slice(FIRST[h], FIRST[h] + ROWS[h])
                out[i, rows, 0:LANES] = decode(main)
                out[i, rows, LANES:2 * LANES] = decode(unfold(shared, h))
            return carry

        lax.fori_loop(0, 4, one, 0)

    def flat(ref, first, rows):
        return ref[first:first + rows].reshape(rows, KX)

    block = s_raw.shape[0] // 4
    fetch[0].wait()
    for m in range(4):
        g_ref[m, SUB - 16:SUB] = jnp.zeros((16, KX), jnp.bfloat16)
        g_ref[m, 0:block] = flat(g_raw, block * m, block)
    pl.semaphore_wait(barrier, 15 - same_core.astype(jnp.int32))

    def window(first, size):
        wide = LANES * (size // LANES + 2)
        base = pl.multiple_of(first // LANES * LANES, LANES)
        return pltpu.roll(levels[:, pl.ds(base, wide)], (wide - first % LANES) % wide, 1)

    def weigh():
        levels[...] = jnp.zeros_like(levels)
        levels[0:1, 0:energies.shape[1]] = energies[...]
        levels[1:2, 0:energies.shape[1]] = occupied[...].astype(jnp.float32)
        n = 4 * block
        across = window(n * col, n)[:, :n]
        down = window(block * (4 * row + aux), block)[:, :2 * LANES].T[:block]
        full, filled = down[:, 1:2], across[1:2]
        pairs = full + filled - 2.0 * full * filled
        weight[...] = -pairs / (4.0 * jnp.abs(down[:, 0:1] - across[0:1]) + 0.5)

    def finish():
        lines = [slice(FIRST[h], FIRST[h] + min(ROWS[h] - 1, block - FIRST[h] + h)) for h in range(2)]
        mine = jnp.concatenate([direct[m, :, :block] for m in range(4)], axis=1)
        turned = [mirror[r].T[:block] for r in range(4)]
        theirs = jnp.concatenate([t[:, part] for t in turned for part in lines], axis=1)
        mine = jnp.concatenate([mine[part] for part in lines], axis=0)
        gradient[...] = mine - theirs

    for d in (1, 3, 2):
        put(a2a[d], g_ref.at[(x + d) % 4], piece(c, 0, 4 - d), x_at(d))
    gbuf[c, 0, :, 0:KX] = g_ref[x]
    spread(0)
    fetch[1].wait()
    for h in range(2):
        rows = min(ROWS[h] - 1, block - FIRST[h] + h)
        for r in range(4):
            first = 4 * FIRST[h] + ROWS[h] * r
            sbuf[first + ROWS[h] - 16:first + ROWS[h], 0:KX] = jnp.zeros((16, KX), jnp.bfloat16)
            sbuf[first:first + rows, 0:KX] = flat(s_raw, block * r + FIRST[h] - h, rows)
    arrived(1)
    arrived(3)
    send_rows(0)
    weigh()
    relay(0)
    arrived(2)
    relay(3)
    forward_rows(0)
    send_rows(1)
    relay(1)
    relay(2)
    for d in (0, 1, 3):
        crossed(d)
    finish_rows(0)
    multiply(0, c, True, False)
    multiply(0, 1 - c, True, False)
    hop(0, 0)
    for p in (0, 3, 1, 2):
        relay_far(p)
    forward_rows(1)
    multiply(0, c, False, True)
    crossed(2)
    multiply(0, 1 - c, False, True)
    begin(1)
    hop(0, 1)
    finish_rows(1)
    multiply(1, c, True, True)
    multiply(1, 1 - c, True, True)
    begin(2)
    hop(0, 2)
    meet(1)
    hop(0, 3)
    meet(2)
    own(0)
    own(1)
    leave(0)
    own(2)
    leave(1)
    turn(0)
    turn(1)
    swap(0)
    swap(1)
    arrive(0)
    unpack(0)
    arrive(1)
    unpack(1)
    finish()
    for copy in sends:
        copy.wait_send()
    for h in range(2):
        for d in range(4):
            @pl.when((y + d) % 4 != x)
            def _():
                along_x(h, d).wait_send()
        for m in range(4):
            @pl.when(jnp.logical_not(jnp.logical_and(same_core, aux == m)))
            def _():
                along_z(h, m).wait_send()


COPIES = 4 + 16 + 16 + 12 + 7 * len(GROUPS) + 32


def exchange(slabs, gammas, energies, occupied):
    vmem, hbm = pl.BlockSpec(memory_space=pltpu.VMEM), pl.BlockSpec(memory_space=pltpu.HBM)
    block = slabs.shape[0]
    out = jax.ShapeDtypeStruct((block // 4, block), jnp.float32)
    hops = [pltpu.VMEM((2, 4, ROWS[h], last - first), jnp.int16) for h, first, last, _ in GROUPS]
    pieces = [pltpu.VMEM((4, p, LANES), jnp.int16) for p in PACKED]
    return pl.pallas_call(
        kernel,
        out_shape=(out, out),
        in_specs=[hbm, hbm, vmem, vmem],
        out_specs=(vmem, vmem),
        scratch_shapes=[
            pltpu.VMEM((8, -(-energies.shape[1] // LANES) * LANES + 2 * LANES), jnp.float32),
            pltpu.VMEM((4, SUB, 2 * LANES), jnp.float32),
            pltpu.VMEM((4, SUB, 2 * LANES), jnp.float32),
            pltpu.VMEM(slabs.shape, slabs.dtype),
            pltpu.VMEM(gammas.shape, gammas.dtype),
            pltpu.VMEM((4, SUB, KX), jnp.bfloat16),
            pltpu.VMEM((4 * SUB, 4 * KX), jnp.bfloat16),
            pltpu.VMEM((2, 4, SUB, 4 * KX), jnp.bfloat16),
            pltpu.VMEM((4, 2, SUB, WIDE), jnp.float32),
            *hops, *hops,
            *[pltpu.VMEM((r, WIDE), jnp.int16) for r in ROWS],
            *pieces, *pieces, *pieces, *pieces, *pieces,
            pltpu.SemaphoreType.DMA((COPIES,)),
            pltpu.SemaphoreType.DMA((COPIES,)),
            pltpu.SemaphoreType.DMA((10,)),
        ],
        compiler_params=pltpu.CompilerParams(
            collective_id=0, has_side_effects=True, vmem_limit_bytes=53 * 1024 * 1024),
        cost_estimate=pl.CostEstimate(
            flops=2 * 640 * 1280 * 2048, bytes_accessed=4 * 1024 * 1024, transcendentals=0),
    )(slabs, gammas, energies, occupied)


def on_device(slabs, gammas, occupied, energies):
    half, weight = exchange(slabs, gammas, energies[None], occupied[None])
    gradient = 2.0 * half
    return gradient, weight * gradient


def solution(mesh):
    placed = (P("row", "col", "aux"), P("row", "col", "aux"), P(), P())
    return jax.shard_map(
        on_device,
        mesh=mesh,
        in_specs=placed,
        out_specs=(P(("row", "aux"), "col"), P(("row", "aux"), "col")),
        check_vma=False,
    )
```

```python
import jax
import jax.numpy as jnp
from jax import lax
from jax.experimental import pallas as pl
from jax.experimental.pallas import tpu as pltpu
from jax.sharding import PartitionSpec as P

SUB = 160
ROWS = (96, 64)
FIRST = (0, ROWS[0])
LANES = 128
REST = SUB - LANES
WIDE = 4 * SUB
KX = 512
FOLD = tuple(-(-r // 32) * 8 for r in ROWS)
PACKED = tuple(r + -(-f // 16) * 16 for r, f in zip(ROWS, FOLD))
TOP = 32760.0
FINE = 128.0
PLACE = (0, 1, 3, 2)
GROUPS = ((0, 0, 3 * LANES, 1), (0, 3 * LANES, WIDE, 1), (1, 0, WIDE, 0))
SHORT = (1, 2)
MESH = pl.DeviceIdType.MESH


def encode(v):
    last = v.shape[0] - 1
    inside = lax.broadcasted_iota(jnp.int32, v.shape, 0) < last
    size = jnp.where(inside, jnp.abs(v), 0.0)
    largest = jnp.maximum(jnp.max(size, axis=0, keepdims=True), 1e-30)
    scale = jnp.ceil(jnp.log2(largest) * FINE)
    code = (jnp.sqrt(size) * (jnp.exp2(scale * (-0.5 / FINE)) * TOP) + 0.5).astype(jnp.int32)
    code = jnp.where(v < 0.0, -code, code)
    return jnp.where(inside, code, scale.astype(jnp.int32)).astype(jnp.int16)


def decode(code):
    value = code.astype(jnp.int32).astype(jnp.float32)
    root = value * (jnp.exp2(value[value.shape[0] - 1:] * (0.5 / FINE)) * (1.0 / TOP))
    return root * jnp.abs(root)


def fold(rest, t, h):
    size = FOLD[h]
    lane = lax.broadcasted_iota(jnp.int32, (size, LANES), 1)
    out = jnp.zeros((size, LANES), jnp.int32)
    for g in range(4):
        rows = rest[size * g:min(size * (g + 1), ROWS[h])]
        if rows.shape[0] < size:
            rows = jnp.concatenate([rows, jnp.zeros((size - rows.shape[0], LANES), jnp.int32)], axis=0)
        if g != t:
            rows = pltpu.roll(rows, (REST * (g - t)) % LANES, 1)
        out = jnp.where(lane // REST == g, rows, out)
    more = PACKED[h] - ROWS[h] - size
    return jnp.concatenate([out, jnp.zeros((more, LANES), jnp.int32)], axis=0) if more else out


def unfold(codes, h):
    parts = []
    for g in range(4):
        rows = codes[:min(FOLD[h], ROWS[h] - FOLD[h] * g)]
        parts.append(pltpu.roll(rows, LANES - REST * g, 1) if g else rows)
    return jnp.concatenate(parts, axis=0)


def kernel(s_hbm, g_hbm, energies, occupied, gradient, weight, levels, direct, mirror, s_raw, g_raw, g_ref, sbuf, gbuf, fock, *rest):
    n = len(GROUPS)
    outgoing, incoming, rest = rest[:n], rest[n:2 * n], rest[2 * n:]
    reduced, packed, direct_codes, mirror_codes, by_y, by_x = (rest[2 * i:2 * i + 2] for i in range(6))
    send, recv, loc = rest[12:]

    fetch = [pltpu.make_async_copy(src, dst, loc.at[8 + i])
             for i, (src, dst) in enumerate(((g_hbm, g_raw), (s_hbm, s_raw)))]
    for copy in fetch:
        copy.start()

    row, col, aux = lax.axis_index("row"), lax.axis_index("col"), lax.axis_index("aux")
    y, c = row // 2, row % 2
    x, zlo = col // 2, col % 2
    z = 2 * aux + zlo

    def at(row_=row, col_=col, aux_=aux):
        return {"row": row_, "col": col_, "aux": aux_}

    def x_at(d):
        return at(col_=2 * ((x + d) % 4) + zlo)

    def y_at(d):
        return at(row_=2 * ((y + d) % 4) + c)

    def z_at(d):
        there = (z + d) % 8
        return at(col_=2 * x + there % 2, aux_=there // 2)

    def swapped(m):
        return at(2 * y + zlo, 2 * x + c, m)

    other = at(row_=2 * y + (1 - c))
    same_core = zlo == c

    barrier = pltpu.get_barrier_semaphore()

    def greet(dev):
        pl.semaphore_signal(barrier, inc=1, device_id=dev, device_id_type=MESH)

    for dev in (x_at(1), x_at(3), x_at(2), y_at(1), y_at(3), y_at(2), other, z_at(1), z_at(7), z_at(2), z_at(6)):
        greet(dev)
    for r in range(4):
        @pl.when(jnp.logical_not(jnp.logical_and(same_core, aux == r)))
        def _():
            greet(swapped(r))

    sends = []
    count = [0]

    def slots(k):
        count[0] += k
        return list(range(count[0] - k, count[0]))

    def remote(n_send, n_recv, src, dst, dev):
        return pltpu.make_async_remote_copy(
            src_ref=src, dst_ref=dst, send_sem=send.at[n_send], recv_sem=recv.at[n_recv],
            device_id=dev, device_id_type=MESH)

    def put(n, src, dst, dev):
        copy = remote(n, n, src, dst, dev)
        copy.start()
        sends.append(copy)

    def got(n, dst, dev):
        remote(n, n, dst, dst, dev).wait_recv()

    lanes = [pl.ds(KX * p, KX) for p in range(4)]

    a2a, cross = slots(4), [slots(4) for _ in range(4)]
    g_out = [slots(4) for _ in range(4)]

    def piece(core, d, p):
        return gbuf.at[core, PLACE[d % 4], :, lanes[p]]

    def over(d, p):
        put(cross[d][p], piece(c, d, p), piece(c, d, p), other)

    def spread(p):
        for d in (1, 3):
            put(g_out[p][d], piece(c, 0, p), piece(c, 4 - d, p), y_at(d))
        over(0, p)

    def arrived(d):
        p = (4 - d) % 4
        got(a2a[d], piece(c, 0, p), x_at(4 - d))
        spread(p)

    def relay(p):
        for d in (3, 1):
            here = piece(c, d, p)
            got(g_out[p][4 - d], here, y_at(d))
            if d == (3 if p in (0, 1) else 1):
                put(g_out[p][2], here, piece(c, 2, p), y_at(4 - d))
            over(d, p)

    def relay_far(p):
        got(g_out[p][2], piece(c, 2, p), y_at(3 if p in (0, 1) else 1))
        over(2, p)

    def crossed(d):
        for p in range(4):
            got(cross[d][p], piece(1 - c, d, p), other)

    s_out, s_far = [slots(4) for _ in ROWS], [slots(2) for _ in ROWS]

    def half_rows(h, i):
        return pl.ds(4 * FIRST[h] + 2 * ROWS[h] * i, 2 * ROWS[h])

    def send_rows(h):
        for part in range(2):
            for i, d in enumerate((1, 3)):
                rows = half_rows(h, (i + part) % 2)
                put(s_out[h][2 * i + part], sbuf.at[rows, lanes[0]], sbuf.at[rows, lanes[4 - d]], x_at(d))

    def near_rows(h, part):
        for i, d in enumerate((1, 3)):
            rows = half_rows(h, (i + part) % 2)
            got(s_out[h][2 * i + part], sbuf.at[rows, lanes[4 - d]], x_at(4 - d))
            if part == 0:
                put(s_far[h][i], sbuf.at[rows, lanes[4 - d]], sbuf.at[rows, lanes[2]], x_at(d))

    def forward_rows(h):
        near_rows(h, 0)

    def finish_rows(h):
        near_rows(h, 1)
        for i, d in enumerate((1, 3)):
            got(s_far[h][i], sbuf.at[half_rows(h, i), lanes[2]], x_at(4 - d))

    def multiply(h, core, near, far):
        a = sbuf[4 * FIRST[h]:4 * (FIRST[h] + ROWS[h])]

        def block(b, first, size):
            out = lax.dot_general(a, b, (((1,), (1,)), ((), ())), preferred_element_type=jnp.float32)
            fock[:, core, FIRST[h]:FIRST[h] + ROWS[h], first:first + size] = out.reshape(4, ROWS[h], size)

        if near and far:
            block(gbuf[core, :, 0:LANES].reshape(4 * LANES, 4 * KX), 0, 4 * LANES)
        elif near:
            block(gbuf[core, 0:3, 0:LANES].reshape(3 * LANES, 4 * KX), 0, 3 * LANES)
        elif far:
            block(gbuf[core, 3, 0:LANES], 3 * LANES, LANES)
        if far:
            block(gbuf[core, :, LANES:SUB].reshape(4 * REST, 4 * KX), 4 * LANES, 4 * REST)

    rs = [[slots(4 if way == longer else 3) for way in range(2)] for _, _, _, longer in GROUPS]

    def sums(k, d, i):
        h, first, _, _ = GROUPS[k]
        there = (z + d) % 8
        return there // 2, there % 2, pl.ds(FIRST[h], ROWS[h]), pl.ds(first + LANES * i, LANES)

    def tiles(k):
        return range((GROUPS[k][2] - GROUPS[k][1]) // LANES)

    def hop(k, step):
        for way in range(2):
            hops = len(rs[k][way])
            if step >= hops:
                continue
            sign = 1 if way == 0 else 7
            if step > 0:
                got(rs[k][way][step - 1], incoming[k].at[way, step - 1], z_at(8 - sign))
            for i in tiles(k):
                cols = pl.ds(LANES * i, LANES)
                v = fock[sums(k, sign * (hops - step), i)]
                if step > 0:
                    v += decode(incoming[k][way, step - 1, :, cols])
                outgoing[k][way, step, :, cols] = encode(v)
            put(rs[k][way][step], outgoing[k].at[way, step], incoming[k].at[way, step], z_at(sign))

    AWAY = (3, 1, 2, 4)
    REACH = (1, 1, 2, 2)

    def message(k, way, n, others):
        sign = 1 if way == 0 else 7
        for i in tiles(k):
            cols = pl.ds(LANES * i, LANES)
            v = fock[sums(k, sign * AWAY[n], i)]
            for m in others:
                v += decode(incoming[k][way, m, :, cols])
            outgoing[k][way, n, :, cols] = encode(v)
        put(rs[k][way][n], outgoing[k].at[way, n], incoming[k].at[way, n], z_at(sign * REACH[n]))

    def came(k, way, n):
        sign = 1 if way == 0 else 7
        got(rs[k][way][n], incoming[k].at[way, n], z_at((8 - sign) * REACH[n]))

    def begin(k):
        for n in (3, 0, 1):
            for way in range(2):
                if n < len(rs[k][way]):
                    message(k, way, n, ())

    def meet(k):
        for way in (1, 0):
            others = (0, 3) if len(rs[k][way]) == 4 else (0,)
            for n in others:
                came(k, way, n)
            message(k, way, 2, others)

    def own(k):
        h, first, _, _ = GROUPS[k]
        last = [(1, 2) if k in SHORT else (len(rs[k][way]) - 1,) for way in range(2)]
        for way in range(2):
            for n in last[way]:
                if k in SHORT:
                    came(k, way, n)
                else:
                    got(rs[k][way][n], incoming[k].at[way, n], z_at(7 if way == 0 else 1))
        for i in tiles(k):
            v = fock[sums(k, 0, i)]
            for way in range(2):
                for n in last[way]:
                    v += decode(incoming[k][way, n, :, pl.ds(LANES * i, LANES)])
            reduced[h][:, first + LANES * i:first + LANES * (i + 1)] = encode(v)

    x_out, y_out = [slots(4) for _ in ROWS], [slots(4) for _ in ROWS]
    t_out, m_out = [slots(4) for _ in ROWS], [slots(4) for _ in ROWS]

    def local(n, src, dst):
        return pltpu.make_async_copy(src, dst, loc.at[n])

    def leave(h):
        shared = reduced[h][:, 4 * LANES:].astype(jnp.int32)
        for d in (2, 1, 3, 0):
            t = PLACE[d]
            packed[h][d, 0:ROWS[h]] = reduced[h][:, LANES * t:LANES * (t + 1)]
            packed[h][d, ROWS[h]:PACKED[h]] = fold(shared, t, h).astype(jnp.int16)
            if d:
                put(y_out[h][d], packed[h].at[d], by_y[h].at[y], y_at(d))
        for d in (2, 1, 3):
            put(x_out[h][d], packed[h].at[(x + d - y + 4) % 4], direct_codes[h].at[x], x_at(d))
        copies = (local(4 * h, packed[h].at[0], by_y[h].at[y]),
                  local(4 * h + 1, packed[h].at[(x - y + 4) % 4], direct_codes[h].at[x]))
        for copy in copies:
            copy.start()
        for copy in copies:
            copy.wait()

    def along_x(h, d):
        t = (y + d) % 4
        return remote(t_out[h][d], t_out[h][0] + x, by_y[h].at[t], by_x[h].at[x], at(col_=2 * t + zlo))

    def along_z(h, m):
        return remote(m_out[h][m], m_out[h][0] + aux, by_x[h].at[m], mirror_codes[h].at[aux], swapped(m))

    def turn(h):
        for d in (0, 1, 3, 2):
            t = (y + d) % 4
            if d:
                got(y_out[h][4 - d], by_y[h].at[t], y_at(d))

            @pl.when(t == x)
            def _():
                copy = local(4 * h + 2, by_y[h].at[t], by_x[h].at[x])
                copy.start()
                copy.wait()

            @pl.when(t != x)
            def _():
                along_x(h, d).start()

    def swap(h):
        for m in range(4):
            @pl.when(m != x)
            def _():
                got(t_out[h][m], by_x[h].at[m], at(col_=2 * m + zlo))

            here = jnp.logical_and(same_core, aux == m)

            @pl.when(here)
            def _():
                copy = local(4 * h + 3, by_x[h].at[m], mirror_codes[h].at[aux])
                copy.start()
                copy.wait()

            @pl.when(jnp.logical_not(here))
            def _():
                along_z(h, m).start()

    def arrive(h):
        for d in (1, 2, 3):
            got(x_out[h][d], direct_codes[h].at[(x + 4 - d) % 4], x_at(4 - d))
        for r in range(4):
            @pl.when(jnp.logical_not(jnp.logical_and(same_core, aux == r)))
            def _():
                got(m_out[h][r], mirror_codes[h].at[r], swapped(r))

    def unpack(h):
        def one(i, carry):
            for codes, out in ((direct_codes[h], direct), (mirror_codes[h], mirror)):
                main, shared = codes[i, 0:ROWS[h]], codes[i, ROWS[h]:PACKED[h]].astype(jnp.int32)
                rows = slice(FIRST[h], FIRST[h] + ROWS[h])
                out[i, rows, 0:LANES] = decode(main)
                out[i, rows, LANES:2 * LANES] = decode(unfold(shared, h))
            return carry

        lax.fori_loop(0, 4, one, 0)

    def flat(ref, first, rows):
        return ref[first:first + rows].reshape(rows, KX)

    block = s_raw.shape[0] // 4
    fetch[0].wait()
    for m in range(4):
        g_ref[m, SUB - 16:SUB] = jnp.zeros((16, KX), jnp.bfloat16)
        g_ref[m, 0:block] = flat(g_raw, block * m, block)
    pl.semaphore_wait(barrier, 15 - same_core.astype(jnp.int32))

    def window(first, size):
        wide = LANES * (size // LANES + 2)
        base = pl.multiple_of(first // LANES * LANES, LANES)
        return pltpu.roll(levels[:, pl.ds(base, wide)], (wide - first % LANES) % wide, 1)

    def weigh():
        levels[...] = jnp.zeros_like(levels)
        levels[0:1, 0:energies.shape[1]] = energies[...]
        levels[1:2, 0:energies.shape[1]] = occupied[...].astype(jnp.float32)
        n = 4 * block
        across = window(n * col, n)[:, :n]
        down = window(block * (4 * row + aux), block)[:, :2 * LANES].T[:block]
        full, filled = down[:, 1:2], across[1:2]
        pairs = full + filled - 2.0 * full * filled
        weight[...] = -pairs / (4.0 * jnp.abs(down[:, 0:1] - across[0:1]) + 0.5)

    def finish():
        lines = [slice(FIRST[h], FIRST[h] + min(ROWS[h] - 1, block - FIRST[h] + h)) for h in range(2)]
        mine = jnp.concatenate([direct[m, :, :block] for m in range(4)], axis=1)
        turned = [mirror[r].T[:block] for r in range(4)]
        theirs = jnp.concatenate([t[:, part] for t in turned for part in lines], axis=1)
        mine = jnp.concatenate([mine[part] for part in lines], axis=0)
        gradient[...] = mine - theirs

    for d in (1, 3, 2):
        put(a2a[d], g_ref.at[(x + d) % 4], piece(c, 0, 4 - d), x_at(d))
    gbuf[c, 0, :, 0:KX] = g_ref[x]
    spread(0)
    fetch[1].wait()
    for h in range(2):
        rows = min(ROWS[h] - 1, block - FIRST[h] + h)
        for r in range(4):
            first = 4 * FIRST[h] + ROWS[h] * r
            sbuf[first + ROWS[h] - 16:first + ROWS[h], 0:KX] = jnp.zeros((16, KX), jnp.bfloat16)
            sbuf[first:first + rows, 0:KX] = flat(s_raw, block * r + FIRST[h] - h, rows)
    arrived(1)
    arrived(3)
    send_rows(0)
    weigh()
    relay(0)
    arrived(2)
    relay(3)
    forward_rows(0)
    send_rows(1)
    relay(1)
    relay(2)
    for d in (0, 1, 3):
        crossed(d)
    finish_rows(0)
    multiply(0, c, True, False)
    multiply(0, 1 - c, True, False)
    hop(0, 0)
    for p in (0, 3, 1, 2):
        relay_far(p)
    forward_rows(1)
    multiply(0, c, False, True)
    crossed(2)
    multiply(0, 1 - c, False, True)
    hop(0, 1)
    begin(1)
    finish_rows(1)
    multiply(1, c, True, True)
    hop(0, 2)
    multiply(1, 1 - c, True, True)
    begin(2)
    meet(1)
    hop(0, 3)
    meet(2)
    own(0)
    own(1)
    leave(0)
    own(2)
    leave(1)
    turn(0)
    turn(1)
    swap(0)
    swap(1)
    arrive(0)
    unpack(0)
    arrive(1)
    unpack(1)
    finish()
    for copy in sends:
        copy.wait_send()
    for h in range(2):
        for d in range(4):
            @pl.when((y + d) % 4 != x)
            def _():
                along_x(h, d).wait_send()
        for m in range(4):
            @pl.when(jnp.logical_not(jnp.logical_and(same_core, aux == m)))
            def _():
                along_z(h, m).wait_send()


COPIES = 4 + 16 + 16 + 12 + 7 * len(GROUPS) + 32


def exchange(slabs, gammas, energies, occupied):
    vmem, hbm = pl.BlockSpec(memory_space=pltpu.VMEM), pl.BlockSpec(memory_space=pltpu.HBM)
    block = slabs.shape[0]
    out = jax.ShapeDtypeStruct((block // 4, block), jnp.float32)
    hops = [pltpu.VMEM((2, 4, ROWS[h], last - first), jnp.int16) for h, first, last, _ in GROUPS]
    pieces = [pltpu.VMEM((4, p, LANES), jnp.int16) for p in PACKED]
    return pl.pallas_call(
        kernel,
        out_shape=(out, out),
        in_specs=[hbm, hbm, vmem, vmem],
        out_specs=(vmem, vmem),
        scratch_shapes=[
            pltpu.VMEM((8, -(-energies.shape[1] // LANES) * LANES + 2 * LANES), jnp.float32),
            pltpu.VMEM((4, SUB, 2 * LANES), jnp.float32),
            pltpu.VMEM((4, SUB, 2 * LANES), jnp.float32),
            pltpu.VMEM(slabs.shape, slabs.dtype),
            pltpu.VMEM(gammas.shape, gammas.dtype),
            pltpu.VMEM((4, SUB, KX), jnp.bfloat16),
            pltpu.VMEM((4 * SUB, 4 * KX), jnp.bfloat16),
            pltpu.VMEM((2, 4, SUB, 4 * KX), jnp.bfloat16),
            pltpu.VMEM((4, 2, SUB, WIDE), jnp.float32),
            *hops, *hops,
            *[pltpu.VMEM((r, WIDE), jnp.int16) for r in ROWS],
            *pieces, *pieces, *pieces, *pieces, *pieces,
            pltpu.SemaphoreType.DMA((COPIES,)),
            pltpu.SemaphoreType.DMA((COPIES,)),
            pltpu.SemaphoreType.DMA((10,)),
        ],
        compiler_params=pltpu.CompilerParams(
            collective_id=0, has_side_effects=True, vmem_limit_bytes=53 * 1024 * 1024),
        cost_estimate=pl.CostEstimate(
            flops=2 * 640 * 1280 * 2048, bytes_accessed=4 * 1024 * 1024, transcendentals=0),
    )(slabs, gammas, energies, occupied)


def on_device(slabs, gammas, occupied, energies):
    half, weight = exchange(slabs, gammas, energies[None], occupied[None])
    gradient = 2.0 * half
    return gradient, weight * gradient


def solution(mesh):
    placed = (P("row", "col", "aux"), P("row", "col", "aux"), P(), P())
    return jax.shard_map(
        on_device,
        mesh=mesh,
        in_specs=placed,
        out_specs=(P(("row", "aux"), "col"), P(("row", "aux"), "col")),
        check_vma=False,
    )
```

```python
import jax
import jax.numpy as jnp
from jax import lax
from jax.experimental import pallas as pl
from jax.experimental.pallas import tpu as pltpu
from jax.sharding import PartitionSpec as P

SUB = 160
ROWS = (96, 64)
FIRST = (0, ROWS[0])
LANES = 128
REST = SUB - LANES
WIDE = 4 * SUB
KX = 512
FOLD = tuple(-(-r // 32) * 8 for r in ROWS)
PACKED = tuple(r + -(-f // 16) * 16 for r, f in zip(ROWS, FOLD))
TOP = 32760.0
FINE = 128.0
PLACE = (0, 1, 3, 2)
GROUPS = ((0, 0, 3 * LANES, 1), (0, 3 * LANES, WIDE, 1), (1, 0, WIDE, 0))
SHORT = (1, 2)
MESH = pl.DeviceIdType.MESH


def encode(v):
    last = v.shape[0] - 1
    inside = lax.broadcasted_iota(jnp.int32, v.shape, 0) < last
    size = jnp.where(inside, jnp.abs(v), 0.0)
    largest = jnp.maximum(jnp.max(size, axis=0, keepdims=True), 1e-30)
    scale = jnp.ceil(jnp.log2(largest) * FINE)
    code = (jnp.sqrt(size) * (jnp.exp2(scale * (-0.5 / FINE)) * TOP) + 0.5).astype(jnp.int32)
    code = jnp.where(v < 0.0, -code, code)
    return jnp.where(inside, code, scale.astype(jnp.int32)).astype(jnp.int16)


def decode(code):
    value = code.astype(jnp.int32).astype(jnp.float32)
    root = value * (jnp.exp2(value[value.shape[0] - 1:] * (0.5 / FINE)) * (1.0 / TOP))
    return root * jnp.abs(root)


def fold(rest, t, h):
    size = FOLD[h]
    lane = lax.broadcasted_iota(jnp.int32, (size, LANES), 1)
    out = jnp.zeros((size, LANES), jnp.int32)
    for g in range(4):
        rows = rest[size * g:min(size * (g + 1), ROWS[h])]
        if rows.shape[0] < size:
            rows = jnp.concatenate([rows, jnp.zeros((size - rows.shape[0], LANES), jnp.int32)], axis=0)
        if g != t:
            rows = pltpu.roll(rows, (REST * (g - t)) % LANES, 1)
        out = jnp.where(lane // REST == g, rows, out)
    more = PACKED[h] - ROWS[h] - size
    return jnp.concatenate([out, jnp.zeros((more, LANES), jnp.int32)], axis=0) if more else out


def unfold(codes, h):
    parts = []
    for g in range(4):
        rows = codes[:min(FOLD[h], ROWS[h] - FOLD[h] * g)]
        parts.append(pltpu.roll(rows, LANES - REST * g, 1) if g else rows)
    return jnp.concatenate(parts, axis=0)


def kernel(s_hbm, g_hbm, pairs, gradient, weight, levels, direct, mirror, s_raw, g_raw, g_ref, sbuf, gbuf, fock, *rest):
    n = len(GROUPS)
    outgoing, incoming, rest = rest[:n], rest[n:2 * n], rest[2 * n:]
    reduced, packed, direct_codes, mirror_codes, by_y, by_x = (rest[2 * i:2 * i + 2] for i in range(6))
    send, recv, loc = rest[12:]

    fetch = [pltpu.make_async_copy(src, dst, loc.at[8 + i])
             for i, (src, dst) in enumerate(((g_hbm, g_raw), (s_hbm, s_raw)))]
    for copy in fetch:
        copy.start()

    row, col, aux = lax.axis_index("row"), lax.axis_index("col"), lax.axis_index("aux")
    y, c = row // 2, row % 2
    x, zlo = col // 2, col % 2
    z = 2 * aux + zlo

    def at(row_=row, col_=col, aux_=aux):
        return {"row": row_, "col": col_, "aux": aux_}

    def x_at(d):
        return at(col_=2 * ((x + d) % 4) + zlo)

    def y_at(d):
        return at(row_=2 * ((y + d) % 4) + c)

    def z_at(d):
        there = (z + d) % 8
        return at(col_=2 * x + there % 2, aux_=there // 2)

    def swapped(m):
        return at(2 * y + zlo, 2 * x + c, m)

    other = at(row_=2 * y + (1 - c))
    same_core = zlo == c

    barrier = pltpu.get_barrier_semaphore()

    def greet(dev):
        pl.semaphore_signal(barrier, inc=1, device_id=dev, device_id_type=MESH)

    for dev in (x_at(1), x_at(3), x_at(2), y_at(1), y_at(3), y_at(2), other, z_at(1), z_at(7), z_at(2), z_at(6)):
        greet(dev)
    for r in range(4):
        @pl.when(jnp.logical_not(jnp.logical_and(same_core, aux == r)))
        def _():
            greet(swapped(r))

    sends = []
    count = [0]

    def slots(k):
        count[0] += k
        return list(range(count[0] - k, count[0]))

    def remote(n_send, n_recv, src, dst, dev):
        return pltpu.make_async_remote_copy(
            src_ref=src, dst_ref=dst, send_sem=send.at[n_send], recv_sem=recv.at[n_recv],
            device_id=dev, device_id_type=MESH)

    def put(n, src, dst, dev):
        copy = remote(n, n, src, dst, dev)
        copy.start()
        sends.append(copy)

    def got(n, dst, dev):
        remote(n, n, dst, dst, dev).wait_recv()

    lanes = [pl.ds(KX * p, KX) for p in range(4)]

    a2a, cross = slots(4), [slots(4) for _ in range(4)]
    g_out = [slots(4) for _ in range(4)]

    def piece(core, d, p):
        return gbuf.at[core, PLACE[d % 4], :, lanes[p]]

    def over(d, p):
        put(cross[d][p], piece(c, d, p), piece(c, d, p), other)

    def spread(p):
        for d in (1, 3):
            put(g_out[p][d], piece(c, 0, p), piece(c, 4 - d, p), y_at(d))
        over(0, p)

    def arrived(d):
        p = (4 - d) % 4
        got(a2a[d], piece(c, 0, p), x_at(4 - d))
        spread(p)

    def relay(p):
        for d in (3, 1):
            here = piece(c, d, p)
            got(g_out[p][4 - d], here, y_at(d))
            if d == (3 if p in (0, 1) else 1):
                put(g_out[p][2], here, piece(c, 2, p), y_at(4 - d))
            over(d, p)

    def relay_far(p):
        got(g_out[p][2], piece(c, 2, p), y_at(3 if p in (0, 1) else 1))
        over(2, p)

    def crossed(d):
        for p in range(4):
            got(cross[d][p], piece(1 - c, d, p), other)

    s_out, s_far = [slots(4) for _ in ROWS], [slots(2) for _ in ROWS]

    def half_rows(h, i):
        return pl.ds(4 * FIRST[h] + 2 * ROWS[h] * i, 2 * ROWS[h])

    def send_rows(h):
        for part in range(2):
            for i, d in enumerate((1, 3)):
                rows = half_rows(h, (i + part) % 2)
                put(s_out[h][2 * i + part], sbuf.at[rows, lanes[0]], sbuf.at[rows, lanes[4 - d]], x_at(d))

    def near_rows(h, part):
        for i, d in enumerate((1, 3)):
            rows = half_rows(h, (i + part) % 2)
            got(s_out[h][2 * i + part], sbuf.at[rows, lanes[4 - d]], x_at(4 - d))
            if part == 0:
                put(s_far[h][i], sbuf.at[rows, lanes[4 - d]], sbuf.at[rows, lanes[2]], x_at(d))

    def forward_rows(h):
        near_rows(h, 0)

    def finish_rows(h):
        near_rows(h, 1)
        for i, d in enumerate((1, 3)):
            got(s_far[h][i], sbuf.at[half_rows(h, i), lanes[2]], x_at(4 - d))

    def multiply(h, core, near, far):
        a = sbuf[4 * FIRST[h]:4 * (FIRST[h] + ROWS[h])]

        def block(b, first, size):
            out = lax.dot_general(a, b, (((1,), (1,)), ((), ())), preferred_element_type=jnp.float32)
            fock[:, core, FIRST[h]:FIRST[h] + ROWS[h], first:first + size] = out.reshape(4, ROWS[h], size)

        if near and far:
            block(gbuf[core, :, 0:LANES].reshape(4 * LANES, 4 * KX), 0, 4 * LANES)
        elif near:
            block(gbuf[core, 0:3, 0:LANES].reshape(3 * LANES, 4 * KX), 0, 3 * LANES)
        elif far:
            block(gbuf[core, 3, 0:LANES], 3 * LANES, LANES)
        if far:
            block(gbuf[core, :, LANES:SUB].reshape(4 * REST, 4 * KX), 4 * LANES, 4 * REST)

    rs = [[slots(4 if way == longer else 3) for way in range(2)] for _, _, _, longer in GROUPS]

    def sums(k, d, i):
        h, first, _, _ = GROUPS[k]
        there = (z + d) % 8
        return there // 2, there % 2, pl.ds(FIRST[h], ROWS[h]), pl.ds(first + LANES * i, LANES)

    def tiles(k):
        return range((GROUPS[k][2] - GROUPS[k][1]) // LANES)

    def hop(k, step):
        for way in range(2):
            hops = len(rs[k][way])
            if step >= hops:
                continue
            sign = 1 if way == 0 else 7
            if step > 0:
                got(rs[k][way][step - 1], incoming[k].at[way, step - 1], z_at(8 - sign))
            for i in tiles(k):
                cols = pl.ds(LANES * i, LANES)
                v = fock[sums(k, sign * (hops - step), i)]
                if step > 0:
                    v += decode(incoming[k][way, step - 1, :, cols])
                outgoing[k][way, step, :, cols] = encode(v)
            put(rs[k][way][step], outgoing[k].at[way, step], incoming[k].at[way, step], z_at(sign))

    AWAY = (3, 1, 2, 4)
    REACH = (1, 1, 2, 2)

    def message(k, way, n, others):
        sign = 1 if way == 0 else 7
        for i in tiles(k):
            cols = pl.ds(LANES * i, LANES)
            v = fock[sums(k, sign * AWAY[n], i)]
            for m in others:
                v += decode(incoming[k][way, m, :, cols])
            outgoing[k][way, n, :, cols] = encode(v)
        put(rs[k][way][n], outgoing[k].at[way, n], incoming[k].at[way, n], z_at(sign * REACH[n]))

    def came(k, way, n):
        sign = 1 if way == 0 else 7
        got(rs[k][way][n], incoming[k].at[way, n], z_at((8 - sign) * REACH[n]))

    def begin(k):
        for n in (3, 0, 1):
            for way in range(2):
                if n < len(rs[k][way]):
                    message(k, way, n, ())

    def meet(k):
        for way in (1, 0):
            others = (0, 3) if len(rs[k][way]) == 4 else (0,)
            for n in others:
                came(k, way, n)
            message(k, way, 2, others)

    def own(k):
        h, first, _, _ = GROUPS[k]
        last = [(1, 2) if k in SHORT else (len(rs[k][way]) - 1,) for way in range(2)]
        for way in range(2):
            for n in last[way]:
                if k in SHORT:
                    came(k, way, n)
                else:
                    got(rs[k][way][n], incoming[k].at[way, n], z_at(7 if way == 0 else 1))
        for i in tiles(k):
            v = fock[sums(k, 0, i)]
            for way in range(2):
                for n in last[way]:
                    v += decode(incoming[k][way, n, :, pl.ds(LANES * i, LANES)])
            reduced[h][:, first + LANES * i:first + LANES * (i + 1)] = encode(v)

    x_out, y_out = [slots(4) for _ in ROWS], [slots(4) for _ in ROWS]
    t_out, m_out = [slots(4) for _ in ROWS], [slots(4) for _ in ROWS]

    def local(n, src, dst):
        return pltpu.make_async_copy(src, dst, loc.at[n])

    def leave(h):
        shared = reduced[h][:, 4 * LANES:].astype(jnp.int32)
        for d in (2, 1, 3, 0):
            t = PLACE[d]
            packed[h][d, 0:ROWS[h]] = reduced[h][:, LANES * t:LANES * (t + 1)]
            packed[h][d, ROWS[h]:PACKED[h]] = fold(shared, t, h).astype(jnp.int16)
            if d:
                put(y_out[h][d], packed[h].at[d], by_y[h].at[y], y_at(d))
        copy = local(4 * h, packed[h].at[0], by_y[h].at[y])
        copy.start()
        copy.wait()

    def depart(h):
        for d in (2, 1, 3):
            put(x_out[h][d], packed[h].at[(x + d - y + 4) % 4], direct_codes[h].at[x], x_at(d))
        copy = local(4 * h + 1, packed[h].at[(x - y + 4) % 4], direct_codes[h].at[x])
        copy.start()
        copy.wait()

    def along_x(h, d):
        t = (y + d) % 4
        return remote(t_out[h][d], t_out[h][0] + x, by_y[h].at[t], by_x[h].at[x], at(col_=2 * t + zlo))

    def along_z(h, m):
        return remote(m_out[h][m], m_out[h][0] + aux, by_x[h].at[m], mirror_codes[h].at[aux], swapped(m))

    def turn(h):
        for d in (0, 1, 3, 2):
            t = (y + d) % 4
            if d:
                got(y_out[h][4 - d], by_y[h].at[t], y_at(d))

            @pl.when(t == x)
            def _():
                copy = local(4 * h + 2, by_y[h].at[t], by_x[h].at[x])
                copy.start()
                copy.wait()

            @pl.when(t != x)
            def _():
                along_x(h, d).start()

    def swap(h):
        for m in range(4):
            @pl.when(m != x)
            def _():
                got(t_out[h][m], by_x[h].at[m], at(col_=2 * m + zlo))

            here = jnp.logical_and(same_core, aux == m)

            @pl.when(here)
            def _():
                copy = local(4 * h + 3, by_x[h].at[m], mirror_codes[h].at[aux])
                copy.start()
                copy.wait()

            @pl.when(jnp.logical_not(here))
            def _():
                along_z(h, m).start()

    def arrive(h):
        for d in (1, 2, 3):
            got(x_out[h][d], direct_codes[h].at[(x + 4 - d) % 4], x_at(4 - d))
        for r in range(4):
            @pl.when(jnp.logical_not(jnp.logical_and(same_core, aux == r)))
            def _():
                got(m_out[h][r], mirror_codes[h].at[r], swapped(r))

    def unpack(h):
        def one(i, carry):
            for codes, out in ((direct_codes[h], direct), (mirror_codes[h], mirror)):
                main, shared = codes[i, 0:ROWS[h]], codes[i, ROWS[h]:PACKED[h]].astype(jnp.int32)
                rows = slice(FIRST[h], FIRST[h] + ROWS[h])
                out[i, rows, 0:LANES] = decode(main)
                out[i, rows, LANES:2 * LANES] = decode(unfold(shared, h))
            return carry

        lax.fori_loop(0, 4, one, 0)

    def flat(ref, first, rows):
        return ref[first:first + rows].reshape(rows, KX)

    block = s_raw.shape[0] // 4
    fetch[0].wait()
    for m in range(4):
        g_ref[m, SUB - 16:SUB] = jnp.zeros((16, KX), jnp.bfloat16)
        g_ref[m, 0:block] = flat(g_raw, block * m, block)
    pl.semaphore_wait(barrier, 15 - same_core.astype(jnp.int32))

    def window(first, size):
        wide = LANES * (size // LANES + 2)
        base = pl.multiple_of(first // LANES * LANES, LANES)
        return pltpu.roll(levels[:, pl.ds(base, wide)], (wide - first % LANES) % wide, 1)

    def weigh():
        levels[...] = jnp.zeros_like(levels)
        levels[0:2, 0:pairs.shape[1]] = pairs[...]
        n = 4 * block
        across = window(n * col, n)[:, :n]
        down = window(block * (4 * row + aux), block)[:, :2 * LANES].T[:block]
        full, filled = down[:, 1:2], across[1:2]
        mixed = full + filled - 2.0 * full * filled
        weight[...] = -mixed / (4.0 * jnp.abs(down[:, 0:1] - across[0:1]) + 0.5)

    def finish():
        lines = [slice(FIRST[h], FIRST[h] + min(ROWS[h] - 1, block - FIRST[h] + h)) for h in range(2)]
        mine = jnp.concatenate([direct[m, :, :block] for m in range(4)], axis=1)
        turned = [mirror[r].T[:block] for r in range(4)]
        theirs = jnp.concatenate([t[:, part] for t in turned for part in lines], axis=1)
        mine = jnp.concatenate([mine[part] for part in lines], axis=0)
        gradient[...] = mine - theirs

    for d in (1, 3, 2):
        put(a2a[d], g_ref.at[(x + d) % 4], piece(c, 0, 4 - d), x_at(d))
    gbuf[c, 0, :, 0:KX] = g_ref[x]
    spread(0)
    fetch[1].wait()
    for h in range(2):
        rows = min(ROWS[h] - 1, block - FIRST[h] + h)
        for r in range(4):
            first = 4 * FIRST[h] + ROWS[h] * r
            sbuf[first + ROWS[h] - 16:first + ROWS[h], 0:KX] = jnp.zeros((16, KX), jnp.bfloat16)
            sbuf[first:first + rows, 0:KX] = flat(s_raw, block * r + FIRST[h] - h, rows)
    arrived(1)
    arrived(3)
    send_rows(0)
    weigh()
    relay(0)
    arrived(2)
    relay(3)
    forward_rows(0)
    send_rows(1)
    relay(1)
    relay(2)
    for d in (0, 1, 3):
        crossed(d)
    finish_rows(0)
    multiply(0, c, True, False)
    multiply(0, 1 - c, True, False)
    hop(0, 0)
    for p in (0, 3, 1, 2):
        relay_far(p)
    forward_rows(1)
    multiply(0, c, False, True)
    crossed(2)
    multiply(0, 1 - c, False, True)
    hop(0, 1)
    begin(1)
    finish_rows(1)
    multiply(1, c, True, True)
    hop(0, 2)
    multiply(1, 1 - c, True, True)
    begin(2)
    meet(1)
    hop(0, 3)
    meet(2)
    own(0)
    own(1)
    leave(0)
    depart(0)
    own(2)
    leave(1)
    turn(0)
    turn(1)
    depart(1)
    swap(0)
    swap(1)
    arrive(0)
    unpack(0)
    arrive(1)
    unpack(1)
    finish()
    for copy in sends:
        copy.wait_send()
    for h in range(2):
        for d in range(4):
            @pl.when((y + d) % 4 != x)
            def _():
                along_x(h, d).wait_send()
        for m in range(4):
            @pl.when(jnp.logical_not(jnp.logical_and(same_core, aux == m)))
            def _():
                along_z(h, m).wait_send()


COPIES = 4 + 16 + 16 + 12 + 7 * len(GROUPS) + 32


def exchange(slabs, gammas, pairs):
    vmem, hbm = pl.BlockSpec(memory_space=pltpu.VMEM), pl.BlockSpec(memory_space=pltpu.HBM)
    block = slabs.shape[0]
    out = jax.ShapeDtypeStruct((block // 4, block), jnp.float32)
    hops = [pltpu.VMEM((2, 4, ROWS[h], last - first), jnp.int16) for h, first, last, _ in GROUPS]
    pieces = [pltpu.VMEM((4, p, LANES), jnp.int16) for p in PACKED]
    return pl.pallas_call(
        kernel,
        out_shape=(out, out),
        in_specs=[hbm, hbm, vmem],
        out_specs=(vmem, vmem),
        scratch_shapes=[
            pltpu.VMEM((8, -(-pairs.shape[1] // LANES) * LANES + 2 * LANES), jnp.float32),
            pltpu.VMEM((4, SUB, 2 * LANES), jnp.float32),
            pltpu.VMEM((4, SUB, 2 * LANES), jnp.float32),
            pltpu.VMEM(slabs.shape, slabs.dtype),
            pltpu.VMEM(gammas.shape, gammas.dtype),
            pltpu.VMEM((4, SUB, KX), jnp.bfloat16),
            pltpu.VMEM((4 * SUB, 4 * KX), jnp.bfloat16),
            pltpu.VMEM((2, 4, SUB, 4 * KX), jnp.bfloat16),
            pltpu.VMEM((4, 2, SUB, WIDE), jnp.float32),
            *hops, *hops,
            *[pltpu.VMEM((r, WIDE), jnp.int16) for r in ROWS],
            *pieces, *pieces, *pieces, *pieces, *pieces,
            pltpu.SemaphoreType.DMA((COPIES,)),
            pltpu.SemaphoreType.DMA((COPIES,)),
            pltpu.SemaphoreType.DMA((10,)),
        ],
        compiler_params=pltpu.CompilerParams(
            collective_id=0, has_side_effects=True, vmem_limit_bytes=53 * 1024 * 1024),
        cost_estimate=pl.CostEstimate(
            flops=2 * 640 * 1280 * 2048, bytes_accessed=4 * 1024 * 1024, transcendentals=0),
    )(slabs, gammas, pairs)


def on_device(slabs, gammas, occupied, energies):
    half, weight = exchange(slabs, gammas, jnp.stack([energies, occupied.astype(jnp.float32)]))
    gradient = 2.0 * half
    return gradient, weight * gradient


def solution(mesh):
    placed = (P("row", "col", "aux"), P("row", "col", "aux"), P(), P())
    return jax.shard_map(
        on_device,
        mesh=mesh,
        in_specs=placed,
        out_specs=(P(("row", "aux"), "col"), P(("row", "aux"), "col")),
        check_vma=False,
    )
```
